1024 devices in a mesh: dp: 4 (over x_hi), expert: 64 (over z, y), tensor: 4 (over x_lo, core).
Axes of the slice: x: 8 (x_hi: 4, x_lo: 2; x = x_hi * 2 + x_lo), y: 8, z: 8, core: 2. Of those that a mesh axis runs over, the one named last changes fastest.
Arguments:
- grad_out: bfloat16 [40960, 5120], P(('dp', 'expert'), 'tensor'), may hold values from -6 to 6
- expert_ids: int32 [40960, 6], P(('dp', 'expert')), may hold values from 0 to 159, all different within a row
- route_probs: float32 [40960, 6], P(('dp', 'expert')), may hold values from 0.05 to 0.6
- saved_gate: bfloat16 [4, 64, 512, 768], P('dp', 'expert'), may hold values from -0.25 to 2
- w_up: bfloat16 [64, 5120, 768], P('expert', 'tensor'), may hold values from -0.078125 to 0.078125
- w_down: bfloat16 [64, 768, 5120], P('expert', None, 'tensor'), may hold values from -0.21875 to 0.21875
- shared_gate: bfloat16 [40960, 768], P(('dp', 'expert')), may hold values from -0.25 to 2
- shared_up: bfloat16 [5120, 768], P('tensor'), may hold values from -0.078125 to 0.078125
- shared_down: bfloat16 [768, 5120], P(None, 'tensor'), may hold values from -0.21875 to 0.21875
Outputs:
- moe_grad: bfloat16 [40960, 5120], P(('dp', 'expert'), 'tensor')
- shared_grad: bfloat16 [40960, 5120], P(('dp', 'expert'), 'tensor')
The draws below stay inside these ranges and needn't reach their ends.
All inputs are finite; a program needn't handle non-finite values.
Results may differ from the reference program's by a relative error of at most 0.0063.
Values may be sent and summed in bfloat16 or wider, within the bound.
No kernel may reach another device: no remote copies, remote signals or barrier semaphores. Data moves between devices by JAX's collectives and lax.ppermute only.
A program may use at most 32 MiB of HBM per device.

```python
import jax
import jax.numpy as jnp
from jax import lax

D = 5120
ALL_EXPERTS = 160
TOP = 6
FF = 768
FS = 768
TOK_DEV = 160
TOKENS = 40960
EXPERTS = 64
CAP = 8
SLOTS = 512
N_DP = 4


def steps_of(key, dims, shards, least, top_value):
    level, own = 1.0, jax.random.fold_in(key, 6)
    for position, blocks in shards:
        steps = jnp.exp(jax.random.uniform(jax.random.fold_in(own, position), (blocks,), jnp.float32, least / len(shards), top_value / len(shards)))
        level = level * jnp.repeat(steps, dims[position] // blocks).reshape([-1 if axis == position else 1 for axis in range(len(dims))])
    return level


def distinct(own_key, rows, amount, top, lift):
    order = jax.random.permutation(jax.random.fold_in(own_key, 1), amount)
    boost = order
    for power in range(3):
        boost = boost * boost // amount
    boost = boost * lift // amount
    chance = jax.random.randint(jax.random.fold_in(own_key, 2), (rows, amount), 0, 4096) + boost
    fixed_rows = jax.random.permutation(jax.random.fold_in(own_key, 3), rows)[jnp.arange(amount) % rows]
    chance = jnp.where(jnp.arange(rows)[:, None] == fixed_rows[None, :], 1 << 14, chance)
    score = chance * amount + jnp.arange(amount)
    return lax.top_k(score.astype(jnp.int32), top)[1].astype(jnp.int32)


def gaussian(rng, extent, spread, bound, pieces=(), kind=jnp.bfloat16):
    factor_of = steps_of(rng, extent, pieces, -0.22, 0.18) if pieces else 1.0
    values = jax.random.normal(rng, extent, jnp.float32) * spread * factor_of
    return jnp.minimum(jnp.maximum(values, -bound), bound).astype(kind)


def setup_inputs(seed: int = 0) -> dict:
    key_of = jax.random.split(jax.random.key(seed), 10)
    return {
        "grad_out": gaussian(key_of[0], (TOKENS, D), 1.0, 6.0, ((0, 256), (1, 4))),
        "expert_ids": distinct(key_of[1], TOKENS, ALL_EXPERTS, TOP, 614),
        "route_probs": jnp.clip(0.05 + 0.55 * jax.random.uniform(key_of[2], (TOKENS, TOP), jnp.float32) ** steps_of(key_of[2], (TOKENS, TOP), ((0, 256),), -0.2, 0.2), 0.05, 0.6),
        "saved_gate": jnp.clip(-0.25 + 2.25 * jax.random.uniform(key_of[3], (N_DP, EXPERTS, SLOTS, FF), jnp.float32) ** steps_of(key_of[3], (N_DP, EXPERTS, SLOTS, FF), ((0, 4), (1, 64)), -0.2, 0.2), -0.25, 2.0).astype(jnp.bfloat16),
        "w_up": gaussian(key_of[4], (EXPERTS, D, FF), D ** -0.5, 0.078125, ((0, 64), (1, 4))),
        "w_down": gaussian(key_of[5], (EXPERTS, FF, D), FF ** -0.5, 0.21875, ((0, 64), (2, 4))),
        "shared_gate": jnp.clip(-0.25 + 2.25 * jax.random.uniform(key_of[6], (TOKENS, FS), jnp.float32) ** steps_of(key_of[6], (TOKENS, FS), ((0, 256),), -0.2, 0.2), -0.25, 2.0).astype(jnp.bfloat16),
        "shared_up": gaussian(key_of[7], (D, FS), D ** -0.5, 0.078125, ((0, 4),)),
        "shared_down": gaussian(key_of[8], (FS, D), FS ** -0.5, 0.21875, ((1, 4),)),
    }


def slot_dest(ids):
    flat = ids.reshape(-1)
    onehot = (flat[:, None] == jnp.arange(EXPERTS, dtype=jnp.int32)[None, :]).astype(jnp.int32)
    ranks = lax.optimization_barrier(jnp.sum((jnp.cumsum(onehot, axis=0) - 1) * onehot, axis=1))
    kept = (flat < EXPERTS) & (ranks < CAP)
    return jnp.where(kept, flat * CAP + ranks, EXPERTS * CAP).astype(jnp.int32)

def replica_grad(grad_rows, id_rows, prob_rows, gate_rows, w_up, w_down):
    dests = jax.vmap(slot_dest)(id_rows)

    def send_one(index):
        values = (prob_rows[index][:, :, None] * grad_rows[index][:, None, :].astype(jnp.float32)).astype(jnp.bfloat16)
        values = values.reshape(TOK_DEV * TOP, D)
        table = jnp.zeros((EXPERTS * CAP + 1, D), jnp.bfloat16).at[dests[index]].set(values)
        return table[:EXPERTS * CAP]
    sent = lax.map(send_one, jnp.arange(EXPERTS, dtype=jnp.int32))
    sent = sent.reshape(EXPERTS, EXPERTS, CAP, D).transpose(1, 0, 2, 3).reshape(EXPERTS, SLOTS, D)

    def expert_one(index):
        hidden = jnp.dot(sent[index], w_down[index].T, preferred_element_type=jnp.float32)
        up_grad = (hidden * gate_rows[index].astype(jnp.float32)).astype(jnp.bfloat16)
        return jnp.dot(up_grad, w_up[index].T, preferred_element_type=jnp.float32).astype(jnp.bfloat16)
    slot_grad = lax.map(expert_one, jnp.arange(EXPERTS, dtype=jnp.int32))
    back = slot_grad.reshape(EXPERTS, EXPERTS, CAP, D).transpose(1, 0, 2, 3).reshape(EXPERTS, EXPERTS * CAP, D)

    def combine_one(index):
        table = jnp.concatenate([back[index], jnp.zeros((1, D), jnp.bfloat16)], axis=0).astype(jnp.float32)
        picked = table[dests[index]].reshape(TOK_DEV, TOP, D)
        return lax.optimization_barrier(jnp.sum(picked, axis=1)).astype(jnp.bfloat16)
    return lax.map(combine_one, jnp.arange(EXPERTS, dtype=jnp.int32))

def reference(grad_out, expert_ids, route_probs, saved_gate, w_up, w_down, shared_gate, shared_up, shared_down):
    replicas = N_DP
    grads = grad_out.reshape(replicas, EXPERTS, TOK_DEV, D)
    ids = expert_ids.reshape(replicas, EXPERTS, TOK_DEV, TOP)
    probs = route_probs.reshape(replicas, EXPERTS, TOK_DEV, TOP)

    def one_replica(index):
        return replica_grad(grads[index], ids[index], probs[index], saved_gate[index], w_up, w_down)
    moe_grad = lax.map(one_replica, jnp.arange(replicas, dtype=jnp.int32)).reshape(TOKENS, D)
    dense_hidden = jnp.dot(grad_out, shared_down.T, preferred_element_type=jnp.float32)
    dense_up = (dense_hidden * shared_gate.astype(jnp.float32)).astype(jnp.bfloat16)
    shared_grad = jnp.dot(dense_up, shared_up.T, preferred_element_type=jnp.float32).astype(jnp.bfloat16)
    return (moe_grad, shared_grad)
```

```python
import jax
import jax.numpy as jnp
from jax import lax
from jax.sharding import PartitionSpec as P

TOP = 6
CAP = 8
CORE_SWAP = [(0, 1), (1, 0), (2, 3), (3, 2)]
CHIP_SWAP = [(0, 2), (1, 3), (2, 0), (3, 1)]


def dot(a, b, dims):
    return lax.dot_general(a, b, (dims, ((), ())), preferred_element_type=jnp.float32)


def pair_sum(part):
    core = lax.axis_index("tensor") % 2
    half = part.shape[0] // 2
    mine = lax.dynamic_slice_in_dim(part, core * half, half)
    other = lax.dynamic_slice_in_dim(part, (1 - core) * half, half)
    chip = mine + lax.ppermute(other, "tensor", CORE_SWAP)
    away = lax.ppermute(chip.astype(jnp.bfloat16), "tensor", CHIP_SWAP)
    return chip + away.astype(jnp.float32)


def both_halves(rows):
    core = lax.axis_index("tensor") % 2
    other = lax.ppermute(rows, "tensor", CORE_SWAP)
    low = jnp.where(core == 0, rows, other)
    high = jnp.where(core == 0, other, rows)
    return jnp.concatenate([low, high], axis=0)


def gated(part, gate):
    core = lax.axis_index("tensor") % 2
    half = part.shape[0] // 2
    mine = lax.dynamic_slice_in_dim(gate, core * half, half)
    up = (pair_sum(part) * mine.astype(jnp.float32)).astype(jnp.bfloat16)
    return both_halves(up)


def on_device(
    grad_out, expert_ids, route_probs, saved_gate, w_up, w_down, shared_gate, shared_up, shared_down
):
    experts = lax.axis_size("expert")
    tok_rows, quarter = grad_out.shape
    parts = 2
    cap = CAP // parts
    picks = expert_ids[:, :, None] == jnp.arange(experts, dtype=jnp.int32)[None, None, :]
    named = jnp.any(picks, axis=1)
    prob = jnp.sum(jnp.where(picks, route_probs[:, :, None], 0.0), axis=1)
    earlier = jnp.arange(tok_rows)[None, :] < jnp.arange(tok_rows)[:, None]
    rank = dot(earlier.astype(jnp.bfloat16), named.astype(jnp.bfloat16), ((1,), (0,)))
    rank = jnp.where(named, rank.astype(jnp.int32), CAP)

    masks, arrived = [], []
    for part in range(parts):
        slots = part * cap + jnp.arange(cap, dtype=jnp.int32)
        mask = rank[:, :, None] == slots[None, None, :]
        slot_prob = jnp.sum(jnp.where(mask, prob[:, :, None], 0.0), axis=0).reshape(experts * cap)
        mask = mask.reshape(tok_rows, experts * cap).astype(jnp.bfloat16)
        picked = dot(mask, grad_out, ((0,), (0,)))
        sent = (picked * slot_prob[:, None]).astype(jnp.bfloat16)
        masks.append(mask)
        arrived.append(
            lax.all_to_all(
                sent.reshape(experts, cap, quarter), "expert", split_axis=0, concat_axis=0, tiled=True
            )
        )
    dense_up = gated(dot(grad_out, shared_down, ((1,), (1,))), shared_gate)
    shared_grad = dot(dense_up, shared_up, ((1,), (1,))).astype(jnp.bfloat16)

    gate = saved_gate[0, 0].reshape(experts, CAP, -1)
    total = None
    for part in range(parts):
        rows = arrived[part].reshape(experts * cap, quarter)
        hidden = dot(rows, w_down[0], ((1,), (1,)))
        gate_rows = gate[:, part * cap : (part + 1) * cap].reshape(experts * cap, -1)
        up_grad = gated(hidden, gate_rows)
        slot_grad = dot(up_grad, w_up[0], ((1,), (1,))).astype(jnp.bfloat16)
        back = lax.all_to_all(
            slot_grad.reshape(experts, cap, quarter), "expert", split_axis=0, concat_axis=0, tiled=True
        )
        term = dot(masks[part], back.reshape(experts * cap, quarter), ((1,), (0,)))
        total = term if total is None else total + term
    return (total.astype(jnp.bfloat16), shared_grad)


def solution(mesh):
    placed = (
        P(("dp", "expert"), "tensor"),
        P(("dp", "expert"), None),
        P(("dp", "expert"), None),
        P("dp", "expert", None, None),
        P("expert", "tensor", None),
        P("expert", None, "tensor"),
        P(("dp", "expert"), None),
        P("tensor", None),
        P(None, "tensor"),
    )
    return jax.shard_map(
        on_device,
        mesh=mesh,
        in_specs=placed,
        out_specs=(P(("dp", "expert"), "tensor"), P(("dp", "expert"), "tensor")),
        check_vma=False,
    )
```

```python
import functools

import jax
import jax.numpy as jnp
from jax import lax
from jax.experimental import pallas as pl
from jax.experimental.pallas import tpu as pltpu
from jax.sharding import PartitionSpec as P

TOP = 6
CAP = 8
CHUNKS = 2
CORE_SWAP = [(0, 1), (1, 0), (2, 3), (3, 2)]
CHIP_SWAP = [(0, 2), (1, 3), (2, 0), (3, 1)]
F32, BF16 = jnp.float32, jnp.bfloat16
WHOLE = pl.BlockSpec(memory_space=pltpu.VMEM)
SCALAR = pl.BlockSpec(memory_space=pltpu.SMEM)


def dot(a, b, dims=((1,), (1,))):
    return lax.dot_general(a, b, (dims, ((), ())), preferred_element_type=F32)


def call(body, outs, specs, scratch=(), flops=0, moved=0):
    return pl.pallas_call(
        body,
        out_shape=outs,
        in_specs=specs,
        out_specs=jax.tree.map(lambda _: WHOLE, outs),
        scratch_shapes=list(scratch),
        compiler_params=pltpu.CompilerParams(vmem_limit_bytes=24 << 20),
        cost_estimate=pl.CostEstimate(flops=flops, bytes_accessed=moved, transcendentals=0),
    )


def route_body(ids_ref, prob_ref, grad_ref, sent_ref, mask_ref, *, experts):
    tokens = ids_ref.shape[1]
    expert = lax.broadcasted_iota(jnp.int32, (experts, tokens), 0)
    named = jnp.zeros((experts, tokens), F32)
    prob = jnp.zeros((experts, tokens), F32)
    for pick in range(TOP):
        hit = ids_ref[pick : pick + 1, :] == expert
        named = jnp.where(hit, 1.0, named)
        prob = jnp.where(hit, prob_ref[pick : pick + 1, :], prob)
    square = (tokens, tokens)
    earlier = lax.broadcasted_iota(jnp.int32, square, 0) < lax.broadcasted_iota(jnp.int32, square, 1)
    rank = dot(named.astype(BF16), jnp.where(earlier, 1.0, 0.0).astype(BF16), ((1,), (0,)))
    rank = jnp.where(named > 0.0, rank, float(CAP))
    shape = (experts, CAP, tokens)
    slot = lax.broadcasted_iota(jnp.int32, shape, 1).astype(F32)
    hit = jnp.broadcast_to(rank[:, None, :], shape) == slot
    scale = jnp.sum(
        jnp.where(hit, jnp.broadcast_to(prob[:, None, :], shape), 0.0), axis=2, keepdims=True
    )
    mask = jnp.where(hit, 1.0, 0.0).reshape(experts * CAP, tokens).astype(BF16)
    mask_ref[...] = mask
    picked = dot(mask, grad_ref[...], ((1,), (0,)))
    sent_ref[...] = (picked * scale.reshape(experts * CAP, 1)).astype(BF16)


def part_body(core_ref, rows_ref, w_ref, mine_ref, other_ref, full_ref, *, first):
    count = full_ref.shape[0]
    half = count // 2
    full_ref[...] = dot(rows_ref[first : first + count, :], w_ref[...])
    mine = pl.multiple_of(core_ref[0] * half, half)
    other = pl.multiple_of((1 - core_ref[0]) * half, half)
    mine_ref[...] = full_ref[pl.ds(mine, half), :]
    other_ref[...] = full_ref[pl.ds(other, half), :]


def gate_body(core_ref, mine_ref, pair_ref, away_ref, gate_ref, up_ref, *, first):
    half = up_ref.shape[0]
    start = pl.multiple_of(first + core_ref[0] * half, 16)
    gate = gate_ref[pl.ds(start, half), :].astype(F32)
    hidden = mine_ref[...] + pair_ref[...] + away_ref[...].astype(F32)
    up_ref[...] = (hidden * gate).astype(BF16)


def up_body(core_ref, *refs):
    *ups, w_ref, out_ref = refs
    half = ups[0].shape[0]
    chunks = len(ups) // 2
    for side in range(2):
        lane = core_ref[0] if side == 0 else 1 - core_ref[0]
        rows = jnp.concatenate([ups[2 * chunk + side][...] for chunk in range(chunks)], axis=0)
        grad = dot(rows, w_ref[...]).astype(BF16)
        for chunk in range(chunks):
            start = pl.multiple_of((2 * chunk + lane) * half, 16)
            out_ref[pl.ds(start, half), :] = grad[chunk * half : (chunk + 1) * half]


def combine_body(mask_ref, back_ref, out_ref):
    out_ref[...] = dot(mask_ref[...], back_ref[...], ((0,), (0,))).astype(BF16)


def tensor_sum(core, parts, gate, count):
    half = count // 2
    width = gate.shape[1]
    pairs = [lax.ppermute(other, "tensor", CORE_SWAP) for _, other in parts]
    aways = [
        lax.ppermute((mine + pair).astype(BF16), "tensor", CHIP_SWAP)
        for (mine, _), pair in zip(parts, pairs)
    ]
    ups = []
    for chunk, ((mine, _), pair, away) in enumerate(zip(parts, pairs, aways)):
        up = call(
            functools.partial(gate_body, first=chunk * count),
            jax.ShapeDtypeStruct((half, width), BF16),
            [SCALAR] + [WHOLE] * 4,
            flops=3 * half * width,
            moved=14 * half * width,
        )(core, mine, pair, away, gate)
        ups += [up, lax.ppermute(up, "tensor", CORE_SWAP)]
    return ups


def partial_rows(core, rows, weight, chunk, count):
    width, depth = weight.shape
    half = jax.ShapeDtypeStruct((count // 2, width), F32)
    return call(
        functools.partial(part_body, first=chunk * count),
        (half, half),
        [SCALAR, WHOLE, WHOLE],
        [pltpu.VMEM((count, width), F32)],
        flops=2 * count * width * depth,
        moved=2 * width * depth,
    )(core, rows, weight)


def up_project(core, ups, weight):
    width, depth = weight.shape
    rows = ups[0].shape[0] * len(ups)
    return call(
        up_body,
        jax.ShapeDtypeStruct((rows, width), BF16),
        [SCALAR] + [WHOLE] * (len(ups) + 1),
        flops=2 * rows * width * depth,
        moved=2 * width * depth,
    )(core, *ups, weight)


def on_device(
    grad_out, expert_ids, route_probs, saved_gate, w_up, w_down, shared_gate, shared_up, shared_down
):
    experts = lax.axis_size("expert")
    tokens, quarter = grad_out.shape
    slots = experts * CAP
    core = (lax.axis_index("tensor") & 1).reshape(1)
    sent, mask = call(
        functools.partial(route_body, experts=experts),
        (
            jax.ShapeDtypeStruct((slots, quarter), BF16),
            jax.ShapeDtypeStruct((slots, tokens), BF16),
        ),
        [WHOLE] * 3,
        flops=2 * slots * tokens * quarter,
        moved=4 * slots * quarter,
    )(expert_ids.T, route_probs.T, grad_out)
    arrived = lax.all_to_all(
        sent.reshape(experts, CAP, quarter), "expert", split_axis=0, concat_axis=0, tiled=True
    ).reshape(slots, quarter)

    dense = [partial_rows(core, grad_out, shared_down, 0, tokens)]
    dense_up = tensor_sum(core, dense, shared_gate, tokens)
    arrived, dense_up = lax.optimization_barrier((arrived, dense_up))
    shared_grad = up_project(core, dense_up, shared_up)

    count = slots // CHUNKS
    parts = [partial_rows(core, arrived, w_down[0], chunk, count) for chunk in range(CHUNKS)]
    ups = tensor_sum(core, parts, saved_gate[0, 0], count)
    slot_grad = up_project(core, ups, w_up[0])
    back = lax.all_to_all(
        slot_grad.reshape(experts, CAP, quarter), "expert", split_axis=0, concat_axis=0, tiled=True
    ).reshape(slots, quarter)
    moe_grad = call(
        combine_body,
        jax.ShapeDtypeStruct((tokens, quarter), BF16),
        [WHOLE, WHOLE],
        flops=2 * slots * tokens * quarter,
        moved=2 * slots * quarter,
    )(mask, back)
    return (moe_grad, shared_grad)


def solution(mesh):
    placed = (
        P(("dp", "expert"), "tensor"),
        P(("dp", "expert"), None),
        P(("dp", "expert"), None),
        P("dp", "expert", None, None),
        P("expert", "tensor", None),
        P("expert", None, "tensor"),
        P(("dp", "expert"), None),
        P("tensor", None),
        P(None, "tensor"),
    )
    return jax.shard_map(
        on_device,
        mesh=mesh,
        in_specs=placed,
        out_specs=(P(("dp", "expert"), "tensor"), P(("dp", "expert"), "tensor")),
        check_vma=False,
    )
```

```python
import functools

import jax
import jax.numpy as jnp
from jax import lax
from jax.experimental import pallas as pl
from jax.experimental.pallas import tpu as pltpu
from jax.sharding import PartitionSpec as P

TOP = 6
CAP = 8
CORES = 2
HELD = CAP // CORES
CORE_SWAP = [(0, 1), (1, 0), (2, 3), (3, 2)]
CHIP_SWAP = [(0, 2), (1, 3), (2, 0), (3, 1)]
F32, BF16 = jnp.float32, jnp.bfloat16
WHOLE = pl.BlockSpec(memory_space=pltpu.VMEM)
FAR = pl.BlockSpec(memory_space=pltpu.HBM)
SCALAR = pl.BlockSpec(memory_space=pltpu.SMEM)


def dot(a, b, dims=((1,), (1,))):
    return lax.dot_general(a, b, (dims, ((), ())), preferred_element_type=F32)


def call(body, outs, specs, scratch=(), flops=0, moved=0):
    return pl.pallas_call(
        body,
        out_shape=outs,
        in_specs=specs,
        out_specs=jax.tree.map(lambda _: WHOLE, outs),
        scratch_shapes=list(scratch),
        compiler_params=pltpu.CompilerParams(vmem_limit_bytes=12 << 20),
        cost_estimate=pl.CostEstimate(flops=flops, bytes_accessed=moved, transcendentals=0),
    )


def low_rows(shape):
    return lax.broadcasted_iota(jnp.int32, shape, len(shape) - 2) < HELD


def route_body(ids_in, prob_in, grad_in, sent_ref, ids_ref, prob_ref, grad_ref, sems, *, experts):
    tokens, quarter = grad_ref.shape
    loads = [
        pltpu.make_async_copy(source, target, sems.at[index])
        for index, (source, target) in enumerate(
            ((ids_in, ids_ref), (prob_in, prob_ref), (grad_in, grad_ref))
        )
    ]
    for load in loads:
        load.start()
    loads[0].wait()
    loads[1].wait()
    expert = lax.broadcasted_iota(jnp.int32, (experts, tokens), 0)
    named = jnp.zeros((experts, tokens), F32)
    prob = jnp.zeros((experts, tokens), F32)
    for pick in range(TOP):
        hit = ids_ref[pick : pick + 1, :] == expert
        named = jnp.where(hit, 1.0, named)
        prob = jnp.where(hit, prob_ref[pick : pick + 1, :], prob)
    square = (tokens, tokens)
    earlier = lax.broadcasted_iota(jnp.int32, square, 0) < lax.broadcasted_iota(jnp.int32, square, 1)
    rank = dot(named.astype(BF16), jnp.where(earlier, 1.0, 0.0).astype(BF16), ((1,), (0,)))
    rank = jnp.where(named > 0.0, rank, float(CAP))
    shape = (experts, CAP, tokens)
    rank = jnp.broadcast_to(rank[:, None, :], shape)
    prob = jnp.broadcast_to(prob[:, None, :], shape)
    slot = lax.rem(lax.broadcasted_iota(jnp.int32, shape, 1), HELD).astype(F32)
    rows, half = experts * CAP, quarter // 2
    loads[2].wait()
    for core in range(CORES):
        hit = rank == slot + float(core * HELD)
        scale = jnp.sum(jnp.where(hit, prob, 0.0), axis=2, keepdims=True)
        mask = jnp.where(hit, 1.0, 0.0).reshape(rows, tokens).astype(BF16)
        left = dot(mask, grad_ref[:, :half], ((1,), (0,))).reshape(experts, CAP, half)
        right = dot(mask, grad_ref[:, half:], ((1,), (0,))).reshape(experts, CAP, half)
        picked = jnp.where(low_rows(left.shape), left, right)
        sent_ref[core] = (picked * scale).astype(BF16)


def mask_body(ids_ref, mask_ref, *, experts):
    tokens = ids_ref.shape[0]
    expert = lax.broadcasted_iota(jnp.int32, (tokens, experts), 1)
    named = jnp.zeros((tokens, experts), F32)
    for pick in range(TOP):
        named = jnp.where(ids_ref[:, pick : pick + 1] == expert, 1.0, named)
    square = (tokens, tokens)
    earlier = lax.broadcasted_iota(jnp.int32, square, 1) < lax.broadcasted_iota(jnp.int32, square, 0)
    rank = dot(jnp.where(earlier, 1.0, 0.0).astype(BF16), named.astype(BF16), ((1,), (0,)))
    rank = jnp.where(named > 0.0, rank, float(CAP)).astype(BF16)
    rows = experts * CAP
    spread = lax.broadcasted_iota(jnp.int32, (experts, rows), 0)
    spread = spread == lax.broadcasted_iota(jnp.int32, (experts, rows), 1) // CAP
    rank = dot(rank, jnp.where(spread, 1.0, 0.0).astype(BF16), ((1,), (0,)))
    slot = lax.rem(lax.broadcasted_iota(jnp.int32, (tokens, rows), 1), HELD).astype(F32)
    for core in range(CORES):
        hit = rank == slot + float(core * HELD)
        mask_ref[:, core * rows : (core + 1) * rows] = jnp.where(hit, 1.0, 0.0).astype(BF16)


def hidden_body(core_ref, rows_ref, mine_ref, other_ref, keep_ref, send_ref):
    total = None
    for lane, w_ref in ((core_ref[0], mine_ref), (1 - core_ref[0], other_ref)):
        rows = rows_ref[lane].astype(F32)
        half = rows.shape[-1]
        pairs = rows.reshape(rows.shape[0] // 2, 2, CAP, half)
        even, odd = pairs[:, 0], pairs[:, 1]
        low = low_rows(even.shape)
        left = jnp.where(low, even, pltpu.roll(odd, HELD, 1))
        right = jnp.where(low, pltpu.roll(even, HELD, 1), odd)
        for column, part in enumerate((left, right)):
            part = part.reshape(-1, half).astype(BF16)
            term = dot(part, w_ref[:, column * half : (column + 1) * half])
            total = term if total is None else total + term
    keep_ref[...] = total
    send_ref[...] = total.astype(BF16)


def slot_grad_body(core_ref, keep_ref, away_ref, gate_ref, mine_ref, other_ref, out_ref):
    hidden = keep_ref[...] + away_ref[...].astype(F32)
    up = (hidden * gate_ref[...].astype(F32)).astype(BF16)
    half = out_ref.shape[-1]
    for lane, w_ref in ((core_ref[0], mine_ref), (1 - core_ref[0], other_ref)):
        left = dot(up, w_ref[:half, :]).reshape(-1, CAP, half)
        right = dot(up, w_ref[half:, :]).reshape(-1, CAP, half)
        low = low_rows(left.shape)
        out_ref[lane, :, 0] = jnp.where(low, left, pltpu.roll(right, HELD, 1)).astype(BF16)
        out_ref[lane, :, 1] = jnp.where(low, pltpu.roll(left, HELD, 1), right).astype(BF16)


def combine_body(mask_in, back_ref, out_ref, mask_ref, sem):
    load = pltpu.make_async_copy(mask_in, mask_ref, sem)
    load.start()
    load.wait()
    half = back_ref.shape[1]
    mask = mask_ref[...]
    low = lax.rem(lax.broadcasted_iota(jnp.int32, mask.shape, 1), CAP) < HELD
    none = jnp.zeros_like(mask)
    left = jnp.where(low, mask, none)
    right = jnp.where(low, none, mask)
    out_ref[:, :half] = dot(left, back_ref[...], ((1,), (0,))).astype(BF16)
    out_ref[:, half:] = dot(right, back_ref[...], ((1,), (0,))).astype(BF16)


def dense_part_body(core_ref, rows_ref, w_ref, mine_ref, other_ref, full_ref):
    half = mine_ref.shape[0]
    full_ref[...] = dot(rows_ref[...], w_ref[...])
    mine_ref[...] = full_ref[pl.ds(pl.multiple_of(core_ref[0] * half, 16), half), :]
    other_ref[...] = full_ref[pl.ds(pl.multiple_of((1 - core_ref[0]) * half, 16), half), :]


def dense_gate_body(core_ref, mine_ref, pair_ref, away_ref, gate_ref, up_ref):
    half = up_ref.shape[0]
    gate = gate_ref[pl.ds(pl.multiple_of(core_ref[0] * half, 16), half), :].astype(F32)
    hidden = mine_ref[...] + pair_ref[...] + away_ref[...].astype(F32)
    up_ref[...] = (hidden * gate).astype(BF16)


def dense_out_body(core_ref, mine_ref, other_ref, w_ref, out_ref):
    half = mine_ref.shape[0]
    grad = dot(jnp.concatenate([mine_ref[...], other_ref[...]], axis=0), w_ref[...]).astype(BF16)
    out_ref[pl.ds(pl.multiple_of(core_ref[0] * half, 16), half), :] = grad[:half]
    out_ref[pl.ds(pl.multiple_of((1 - core_ref[0]) * half, 16), half), :] = grad[half:]


def dense_up_grad(core, grad_out, shared_down, shared_gate):
    tokens, depth = grad_out.shape
    width = shared_down.shape[0]
    half = jax.ShapeDtypeStruct((tokens // 2, width), F32)
    mine, other = call(
        dense_part_body,
        (half, half),
        [SCALAR, WHOLE, WHOLE],
        [pltpu.VMEM((tokens, width), F32)],
        flops=2 * tokens * width * depth,
        moved=2 * width * depth,
    )(core, grad_out, shared_down)
    pair = lax.ppermute(other, "tensor", CORE_SWAP)
    away = lax.ppermute((mine + pair).astype(BF16), "tensor", CHIP_SWAP)
    up = call(
        dense_gate_body,
        jax.ShapeDtypeStruct((tokens // 2, width), BF16),
        [SCALAR] + [WHOLE] * 4,
        flops=3 * tokens * width,
        moved=7 * tokens * width,
    )(core, mine, pair, away, shared_gate)
    return up, lax.ppermute(up, "tensor", CORE_SWAP)


def on_device(
    grad_out, expert_ids, route_probs, saved_gate, w_up, w_down, shared_gate, shared_up, shared_down
):
    experts = lax.axis_size("expert")
    tokens, quarter = grad_out.shape
    half, slots, held = quarter // 2, experts * CAP, experts * HELD
    core = (lax.axis_index("tensor") & 1).reshape(1)
    groups = [
        [place * 4 + chip * 2 + lane for lane in range(CORES) for place in range(experts)]
        for chip in range(2)
    ]

    def exchange(rows):
        rows = rows.reshape(CORES * experts, CAP, half)
        return lax.all_to_all(
            rows, ("expert", "tensor"), 0, 0, axis_index_groups=groups, tiled=True
        )

    ids, probs = expert_ids.T, route_probs.T
    sent = call(
        functools.partial(route_body, experts=experts),
        pltpu.VMEM((CORES, experts, CAP, half), BF16),
        [FAR] * 3,
        [pltpu.VMEM(array.shape, array.dtype) for array in (ids, probs, grad_out)]
        + [pltpu.SemaphoreType.DMA((3,))],
        flops=4 * slots * tokens * quarter,
        moved=4 * slots * quarter,
    )(*(pltpu.with_memory_space_constraint(array, pltpu.HBM) for array in (ids, probs, grad_out)))
    arrived = exchange(sent)

    down_other = lax.ppermute(w_down[0], "tensor", CORE_SWAP)
    up_other = lax.ppermute(w_up[0], "tensor", CORE_SWAP)
    gate = saved_gate.reshape(experts, CORES, HELD, -1)
    gate = lax.dynamic_index_in_dim(gate, core[0], 1, keepdims=False).reshape(held, -1)
    dense_up = dense_up_grad(core, grad_out, shared_down, shared_gate)
    shared_grad = call(
        dense_out_body,
        jax.ShapeDtypeStruct((tokens, quarter), BF16),
        [SCALAR] + [WHOLE] * 3,
        flops=2 * tokens * quarter * shared_up.shape[1],
        moved=2 * quarter * shared_up.shape[1],
    )(core, *dense_up, shared_up)
    mask = call(
        functools.partial(mask_body, experts=experts),
        jax.ShapeDtypeStruct((tokens, CORES * slots), BF16),
        [WHOLE],
        flops=2 * tokens * slots * experts,
        moved=4 * tokens * slots,
    )(expert_ids)
    arrived, down_other, up_other, gate, shared_grad, mask = lax.optimization_barrier(
        (arrived, down_other, up_other, gate, shared_grad, mask)
    )
    work = 4 * held * quarter * gate.shape[1]
    keep, send = call(
        hidden_body,
        (jax.ShapeDtypeStruct(gate.shape, F32), jax.ShapeDtypeStruct(gate.shape, BF16)),
        [SCALAR] + [WHOLE] * 3,
        flops=work,
        moved=4 * quarter * gate.shape[1],
    )(core, arrived.reshape(CORES, experts, CAP, half), w_down[0], down_other)
    away = lax.ppermute(send, "tensor", CHIP_SWAP)
    slot_grad = call(
        slot_grad_body,
        pltpu.VMEM((CORES, experts // 2, 2, CAP, half), BF16),
        [SCALAR] + [WHOLE] * 5,
        flops=work,
        moved=4 * quarter * gate.shape[1],
    )(core, keep, away, gate, w_up[0], up_other)
    back = exchange(slot_grad)
    moe_grad = call(
        combine_body,
        jax.ShapeDtypeStruct((tokens, quarter), BF16),
        [FAR, WHOLE],
        [pltpu.VMEM(mask.shape, BF16), pltpu.SemaphoreType.DMA(())],
        flops=4 * slots * tokens * quarter,
        moved=2 * slots * quarter,
    )(pltpu.with_memory_space_constraint(mask, pltpu.HBM), back.reshape(CORES * slots, half))
    return (moe_grad, shared_grad)


def solution(mesh):
    placed = (
        P(("dp", "expert"), "tensor"),
        P(("dp", "expert"), None),
        P(("dp", "expert"), None),
        P("dp", "expert", None, None),
        P("expert", "tensor", None),
        P("expert", None, "tensor"),
        P(("dp", "expert"), None),
        P("tensor", None),
        P(None, "tensor"),
    )
    return jax.shard_map(
        on_device,
        mesh=mesh,
        in_specs=placed,
        out_specs=(P(("dp", "expert"), "tensor"), P(("dp", "expert"), "tensor")),
        check_vma=False,
    )
```

```python
import functools

import jax
import jax.numpy as jnp
from jax import lax
from jax.experimental import pallas as pl
from jax.experimental.pallas import tpu as pltpu
from jax.sharding import PartitionSpec as P

TOP = 6
CAP = 8
CORES = 2
HELD = CAP // CORES
CORE_SWAP = [(0, 1), (1, 0), (2, 3), (3, 2)]
CHIP_SWAP = [(0, 2), (1, 3), (2, 0), (3, 1)]
F32, BF16 = jnp.float32, jnp.bfloat16
WHOLE = pl.BlockSpec(memory_space=pltpu.VMEM)
FAR = pl.BlockSpec(memory_space=pltpu.HBM)
ANY = pl.BlockSpec(memory_space=pl.ANY)
SCALAR = pl.BlockSpec(memory_space=pltpu.SMEM)


def dot(a, b, dims=((1,), (1,))):
    return lax.dot_general(a, b, (dims, ((), ())), preferred_element_type=F32)


def call(body, outs, specs, scratch=(), flops=0, moved=0):
    return pl.pallas_call(
        body,
        out_shape=outs,
        in_specs=specs,
        out_specs=jax.tree.map(lambda _: WHOLE, outs),
        scratch_shapes=list(scratch),
        compiler_params=pltpu.CompilerParams(vmem_limit_bytes=12 << 20),
        cost_estimate=pl.CostEstimate(flops=flops, bytes_accessed=moved, transcendentals=0),
    )


def far(*arrays):
    return tuple(pltpu.with_memory_space_constraint(array, pltpu.HBM) for array in arrays)


def low_rows(shape):
    return lax.broadcasted_iota(jnp.int32, shape, len(shape) - 2) < HELD


def pack(even, odd, side):
    low = low_rows(even.shape)
    if side == 0:
        return jnp.where(low, even, pltpu.roll(odd, HELD, 1))
    return jnp.where(low, pltpu.roll(even, HELD, 1), odd)


def route_body(ids_in, prob_in, grad_in, sent_ref, ids_ref, prob_ref, grad_ref, sems, *, experts):
    tokens, quarter = grad_ref.shape
    loads = [
        pltpu.make_async_copy(source, target, sems.at[index])
        for index, (source, target) in enumerate(
            ((ids_in, ids_ref), (prob_in, prob_ref), (grad_in, grad_ref))
        )
    ]
    for load in loads:
        load.start()
    loads[0].wait()
    loads[1].wait()
    pairs, half = experts // 2, quarter // 2
    row = lax.broadcasted_iota(jnp.int32, (experts, tokens), 0)
    expert = jnp.where(row < pairs, 2 * row, 2 * (row - pairs) + 1)
    named = jnp.zeros((experts, tokens), F32)
    prob = jnp.zeros((experts, tokens), F32)
    for pick in range(TOP):
        hit = ids_ref[pick : pick + 1, :] == expert
        named = jnp.where(hit, 1.0, named)
        prob = jnp.where(hit, prob_ref[pick : pick + 1, :], prob)
    square = (tokens, tokens)
    earlier = lax.broadcasted_iota(jnp.int32, square, 0) < lax.broadcasted_iota(jnp.int32, square, 1)
    rank = dot(named.astype(BF16), jnp.where(earlier, 1.0, 0.0).astype(BF16), ((1,), (0,)))
    rank = jnp.where(named > 0.0, rank, float(CAP))
    shape = (pairs, CAP, tokens)
    low = low_rows(shape)

    def spread(table):
        even = jnp.broadcast_to(table[:pairs, None, :], shape)
        return jnp.where(low, even, jnp.broadcast_to(table[pairs:, None, :], shape))

    rank, prob = spread(rank), spread(prob)
    slot = lax.rem(lax.broadcasted_iota(jnp.int32, shape, 1), HELD).astype(F32)
    loads[2].wait()
    for core in range(CORES):
        hit = rank == slot + float(core * HELD)
        scale = jnp.sum(jnp.where(hit, prob, 0.0), axis=2, keepdims=True)
        mask = jnp.where(hit, 1.0, 0.0).reshape(pairs * CAP, tokens).astype(BF16)
        left = dot(mask, grad_ref[:, :half], ((1,), (0,))).reshape(pairs, CAP, half) * scale
        right = dot(mask, grad_ref[:, half:], ((1,), (0,))).reshape(pairs, CAP, half) * scale
        sent_ref[core, :, 0] = pack(left, right, 0).astype(BF16)
        sent_ref[core, :, 1] = pack(left, right, 1).astype(BF16)


def prepare_body(ids_ref, after_ref, mine_in, other_in, mask_ref, w_ref, sems, *, experts):
    loads = [
        pltpu.make_async_copy(source, w_ref.at[index], sems.at[index])
        for index, source in enumerate((mine_in, other_in))
    ]
    for load in loads:
        load.start()
    tokens = ids_ref.shape[0]
    expert = lax.broadcasted_iota(jnp.int32, (tokens, experts), 1)
    named = jnp.zeros((tokens, experts), F32)
    for pick in range(TOP):
        named = jnp.where(ids_ref[:, pick : pick + 1] == expert, 1.0, named)
    square = (tokens, tokens)
    earlier = lax.broadcasted_iota(jnp.int32, square, 1) < lax.broadcasted_iota(jnp.int32, square, 0)
    rank = dot(jnp.where(earlier, 1.0, 0.0).astype(BF16), named.astype(BF16), ((1,), (0,)))
    rank = jnp.where(named > 0.0, rank, float(CAP)).astype(BF16)
    rows = experts * CAP
    spread = lax.broadcasted_iota(jnp.int32, (experts, rows), 0)
    spread = spread == lax.broadcasted_iota(jnp.int32, (experts, rows), 1) // CAP
    rank = dot(rank, jnp.where(spread, 1.0, 0.0).astype(BF16), ((1,), (0,)))
    row = lax.broadcasted_iota(jnp.int32, (tokens, rows), 1)
    slot = lax.rem(row, HELD).astype(F32)
    low = lax.rem(row, CAP) < HELD
    for core in range(CORES):
        hit = rank == slot + float(core * HELD)
        columns = slice(core * rows, (core + 1) * rows)
        mask_ref[:tokens, columns] = jnp.where(hit & low, 1.0, 0.0).astype(BF16)
        mask_ref[tokens:, columns] = jnp.where(hit & ~low, 1.0, 0.0).astype(BF16)
    for load in loads:
        load.wait()


def gate_pick_body(core_ref, gate_ref, out_ref):
    rows = gate_ref[...].astype(F32).reshape(-1, 2, CAP, gate_ref.shape[1])
    even, odd = rows[:, 0], rows[:, 1]
    first, last = pack(even, odd, 0), pack(even, odd, 1)
    chosen = jnp.where(core_ref[0] == 0, first, last)
    out_ref[...] = chosen.reshape(out_ref.shape).astype(BF16)


def hidden_body(core_ref, rows_ref, mine_in, other_in, keep_ref, send_ref, w_ref, sems):
    loads = [
        pltpu.make_async_copy(source, w_ref.at[index], sems.at[index])
        for index, source in enumerate((mine_in, other_in))
    ]
    for load in loads:
        load.start()
    total = None
    for index, lane in enumerate((core_ref[0], 1 - core_ref[0])):
        rows = rows_ref[lane].astype(F32)
        half = rows.shape[-1]
        rows = rows.reshape(-1, 2, CAP, half)
        parts = [pack(rows[:, 0], rows[:, 1], side).reshape(-1, half).astype(BF16) for side in range(2)]
        loads[index].wait()
        for side, part in enumerate(parts):
            term = dot(part, w_ref[index, :, side * half : (side + 1) * half])
            total = term if total is None else total + term
    keep_ref[...] = total
    send_ref[...] = total.astype(BF16)


def slot_grad_body(core_ref, keep_ref, away_ref, gate_ref, w_ref, mask_in, out_ref):
    hidden = keep_ref[...] + away_ref[...].astype(F32)
    up = (hidden * gate_ref[...].astype(F32)).astype(BF16)
    half = out_ref.shape[-1]
    for index, lane in enumerate((core_ref[0], 1 - core_ref[0])):
        left = dot(up, w_ref[index, :half, :]).reshape(-1, CAP, half)
        right = dot(up, w_ref[index, half:, :]).reshape(-1, CAP, half)
        out_ref[lane, :, 0] = pack(left, right, 0).astype(BF16)
        out_ref[lane, :, 1] = pack(left, right, 1).astype(BF16)


def combine_body(mask_ref, back_ref, out_ref):
    tokens, half = out_ref.shape[0], back_ref.shape[1]
    both = dot(mask_ref[...], back_ref[...], ((1,), (0,))).astype(BF16)
    out_ref[:, :half] = both[:tokens]
    out_ref[:, half:] = both[tokens:]


def dense_part_body(core_ref, rows_ref, w_ref, mine_ref, other_ref, full_ref):
    half = mine_ref.shape[0]
    full_ref[...] = dot(rows_ref[...], w_ref[...])
    mine_ref[...] = full_ref[pl.ds(pl.multiple_of(core_ref[0] * half, 16), half), :]
    other_ref[...] = full_ref[pl.ds(pl.multiple_of((1 - core_ref[0]) * half, 16), half), :]


def dense_gate_body(core_ref, mine_ref, pair_ref, away_ref, gate_ref, up_ref):
    half = up_ref.shape[0]
    gate = gate_ref[pl.ds(pl.multiple_of(core_ref[0] * half, 16), half), :].astype(F32)
    hidden = mine_ref[...] + pair_ref[...] + away_ref[...].astype(F32)
    up_ref[...] = (hidden * gate).astype(BF16)


def dense_out_body(core_ref, mine_ref, other_ref, w_ref, out_ref):
    half = mine_ref.shape[0]
    grad = dot(jnp.concatenate([mine_ref[...], other_ref[...]], axis=0), w_ref[...]).astype(BF16)
    out_ref[pl.ds(pl.multiple_of(core_ref[0] * half, 16), half), :] = grad[:half]
    out_ref[pl.ds(pl.multiple_of((1 - core_ref[0]) * half, 16), half), :] = grad[half:]


def dense_up_grad(core, grad_out, shared_down, shared_gate):
    tokens, depth = grad_out.shape
    width = shared_down.shape[0]
    half = jax.ShapeDtypeStruct((tokens // 2, width), F32)
    mine, other = call(
        dense_part_body,
        (half, half),
        [SCALAR, WHOLE, WHOLE],
        [pltpu.VMEM((tokens, width), F32)],
        flops=2 * tokens * width * depth,
        moved=2 * width * depth,
    )(core, grad_out, shared_down)
    pair = lax.ppermute(other, "tensor", CORE_SWAP)
    away = lax.ppermute((mine + pair).astype(BF16), "tensor", CHIP_SWAP)
    up = call(
        dense_gate_body,
        jax.ShapeDtypeStruct((tokens // 2, width), BF16),
        [SCALAR] + [WHOLE] * 4,
        flops=3 * tokens * width,
        moved=7 * tokens * width,
    )(core, mine, pair, away, shared_gate)
    return up, lax.ppermute(up, "tensor", CORE_SWAP)


def on_device(
    grad_out, expert_ids, route_probs, saved_gate, w_up, w_down, shared_gate, shared_up, shared_down
):
    experts = lax.axis_size("expert")
    tokens, quarter = grad_out.shape
    half, slots, held = quarter // 2, experts * CAP, experts * HELD
    core = (lax.axis_index("tensor") & 1).reshape(1)
    groups = [
        [place * 4 + chip * 2 + lane for lane in range(CORES) for place in range(experts)]
        for chip in range(2)
    ]

    def exchange(rows):
        rows = rows.reshape(CORES * experts, CAP, half)
        return lax.all_to_all(
            rows, ("expert", "tensor"), 0, 0, axis_index_groups=groups, tiled=True
        )

    ids, probs = expert_ids.T, route_probs.T
    sent = call(
        functools.partial(route_body, experts=experts),
        jax.ShapeDtypeStruct((CORES, experts // 2, 2, CAP, half), BF16),
        [FAR] * 3,
        [pltpu.VMEM(array.shape, array.dtype) for array in (ids, probs, grad_out)]
        + [pltpu.SemaphoreType.DMA((3,))],
        flops=2 * slots * tokens * quarter,
        moved=4 * slots * quarter,
    )(*far(ids, probs, grad_out))
    arrived = exchange(sent)

    down_other = lax.ppermute(w_down[0], "tensor", CORE_SWAP)
    up_other = lax.ppermute(w_up[0], "tensor", CORE_SWAP)
    width = w_down.shape[1]
    gate = call(
        gate_pick_body,
        jax.ShapeDtypeStruct((held, width), BF16),
        [SCALAR, WHOLE],
        flops=slots * width,
        moved=3 * slots * width,
    )(core, saved_gate[0, 0])
    dense_up = dense_up_grad(core, grad_out, shared_down, shared_gate)
    shared_grad = call(
        dense_out_body,
        jax.ShapeDtypeStruct((tokens, quarter), BF16),
        [SCALAR] + [WHOLE] * 3,
        flops=2 * tokens * quarter * shared_up.shape[1],
        moved=2 * quarter * shared_up.shape[1],
    )(core, *dense_up, shared_up)
    ids, arrived, down_other, up_other, gate, shared_grad = lax.optimization_barrier(
        (expert_ids, arrived, down_other, up_other, gate, shared_grad)
    )
    work = 4 * held * quarter * width
    keep, send = call(
        hidden_body,
        (jax.ShapeDtypeStruct(gate.shape, F32), jax.ShapeDtypeStruct(gate.shape, BF16)),
        [SCALAR, WHOLE, FAR, FAR],
        [pltpu.VMEM((CORES, width, quarter), BF16), pltpu.SemaphoreType.DMA((CORES,))],
        flops=work,
        moved=4 * quarter * width,
    )(core, arrived.reshape(CORES, experts, CAP, half), *far(w_down[0], down_other))
    away = lax.ppermute(send, "tensor", CHIP_SWAP)
    mask, w_both = call(
        functools.partial(prepare_body, experts=experts),
        (
            jax.ShapeDtypeStruct((2 * tokens, CORES * slots), BF16),
            jax.ShapeDtypeStruct((CORES, quarter, width), BF16),
        ),
        [WHOLE, ANY, FAR, FAR],
        [pltpu.SemaphoreType.DMA((CORES,))],
        flops=2 * tokens * slots * experts,
        moved=4 * quarter * width,
    )(ids, keep, *far(w_up[0], up_other))
    slot_grad = call(
        slot_grad_body,
        jax.ShapeDtypeStruct((CORES, experts // 2, 2, CAP, half), BF16),
        [SCALAR] + [WHOLE] * 4 + [ANY],
        flops=work,
        moved=4 * quarter * width,
    )(core, keep, away, gate, w_both, mask)
    back = exchange(slot_grad)
    moe_grad = call(
        combine_body,
        jax.ShapeDtypeStruct((tokens, quarter), BF16),
        [WHOLE] * 2,
        flops=4 * slots * tokens * quarter,
        moved=2 * slots * quarter,
    )(mask, back.reshape(CORES * slots, half))
    return (moe_grad, shared_grad)


def solution(mesh):
    placed = (
        P(("dp", "expert"), "tensor"),
        P(("dp", "expert"), None),
        P(("dp", "expert"), None),
        P("dp", "expert", None, None),
        P("expert", "tensor", None),
        P("expert", None, "tensor"),
        P(("dp", "expert"), None),
        P("tensor", None),
        P(None, "tensor"),
    )
    return jax.shard_map(
        on_device,
        mesh=mesh,
        in_specs=placed,
        out_specs=(P(("dp", "expert"), "tensor"), P(("dp", "expert"), "tensor")),
        check_vma=False,
    )
```

```python
import functools

import jax
import jax.numpy as jnp
from jax import lax
from jax.experimental import pallas as pl
from jax.experimental.pallas import tpu as pltpu
from jax.sharding import PartitionSpec as P

TOP = 6
CAP = 8
CORES = 2
HELD = CAP // CORES
CORE_SWAP = [(0, 1), (1, 0), (2, 3), (3, 2)]
CHIP_SWAP = [(0, 2), (1, 3), (2, 0), (3, 1)]
F32, BF16 = jnp.float32, jnp.bfloat16
WHOLE = pl.BlockSpec(memory_space=pltpu.VMEM)
FAR = pl.BlockSpec(memory_space=pltpu.HBM)
SCALAR = pl.BlockSpec(memory_space=pltpu.SMEM)


def dot(a, b, dims=((1,), (1,))):
    return lax.dot_general(a, b, (dims, ((), ())), preferred_element_type=F32)


def call(body, outs, specs, scratch=(), flops=0, moved=0, place=WHOLE):
    return pl.pallas_call(
        body,
        out_shape=outs,
        in_specs=specs,
        out_specs=jax.tree.map(lambda _: place, outs),
        scratch_shapes=list(scratch),
        compiler_params=pltpu.CompilerParams(vmem_limit_bytes=12 << 20),
        cost_estimate=pl.CostEstimate(flops=flops, bytes_accessed=moved, transcendentals=0),
    )


def far(*arrays):
    return tuple(pltpu.with_memory_space_constraint(array, pltpu.HBM) for array in arrays)


def low_rows(shape):
    return lax.broadcasted_iota(jnp.int32, shape, len(shape) - 2) < HELD


def pack(even, odd, side):
    low = low_rows(even.shape)
    if side == 0:
        return jnp.where(low, even, pltpu.roll(odd, HELD, 1))
    return jnp.where(low, pltpu.roll(even, HELD, 1), odd)


def route_body(
    ids_in, prob_in, grad_in, sent_out, ids_ref, prob_ref, grad_ref, sent_ref, sems, *, experts
):
    tokens, quarter = grad_ref.shape
    loads = [
        pltpu.make_async_copy(source, target, sems.at[index])
        for index, (source, target) in enumerate(
            ((ids_in, ids_ref), (prob_in, prob_ref), (grad_in, grad_ref))
        )
    ]
    for load in loads:
        load.start()
    loads[0].wait()
    loads[1].wait()
    pairs, half = experts // 2, quarter // 2
    row = lax.broadcasted_iota(jnp.int32, (experts, tokens), 0)
    expert = jnp.where(row < pairs, 2 * row, 2 * (row - pairs) + 1)
    named = jnp.zeros((experts, tokens), F32)
    prob = jnp.zeros((experts, tokens), F32)
    for pick in range(TOP):
        hit = ids_ref[pick : pick + 1, :] == expert
        named = jnp.where(hit, 1.0, named)
        prob = jnp.where(hit, prob_ref[pick : pick + 1, :], prob)
    square = (tokens, tokens)
    earlier = lax.broadcasted_iota(jnp.int32, square, 0) < lax.broadcasted_iota(jnp.int32, square, 1)
    rank = dot(named.astype(BF16), jnp.where(earlier, 1.0, 0.0).astype(BF16), ((1,), (0,)))
    rank = jnp.where(named > 0.0, rank, float(CAP))
    shape = (pairs, CAP, tokens)
    low = low_rows(shape)

    def spread(table):
        even = jnp.broadcast_to(table[:pairs, None, :], shape)
        return jnp.where(low, even, jnp.broadcast_to(table[pairs:, None, :], shape))

    rank, prob = spread(rank), spread(prob)
    slot = lax.rem(lax.broadcasted_iota(jnp.int32, shape, 1), HELD).astype(F32)
    loads[2].wait()
    stores = [
        pltpu.make_async_copy(sent_ref.at[core], sent_out.at[core], sems.at[3 + core])
        for core in range(CORES)
    ]
    for core in range(CORES):
        hit = rank == slot + float(core * HELD)
        scale = jnp.sum(jnp.where(hit, prob, 0.0), axis=2, keepdims=True)
        mask = jnp.where(hit, 1.0, 0.0).reshape(pairs * CAP, tokens).astype(BF16)
        left = dot(mask, grad_ref[:, :half], ((1,), (0,))).reshape(pairs, CAP, half) * scale
        right = dot(mask, grad_ref[:, half:], ((1,), (0,))).reshape(pairs, CAP, half) * scale
        sent_ref[core, :, 0] = pack(left, right, 0).astype(BF16)
        sent_ref[core, :, 1] = pack(left, right, 1).astype(BF16)
        stores[core].start()
    for store in stores:
        store.wait()


def mask_body(ids_ref, mask_ref, *, experts):
    tokens = ids_ref.shape[0]
    expert = lax.broadcasted_iota(jnp.int32, (tokens, experts), 1)
    named = jnp.zeros((tokens, experts), F32)
    for pick in range(TOP):
        named = jnp.where(ids_ref[:, pick : pick + 1] == expert, 1.0, named)
    square = (tokens, tokens)
    earlier = lax.broadcasted_iota(jnp.int32, square, 1) < lax.broadcasted_iota(jnp.int32, square, 0)
    rank = dot(jnp.where(earlier, 1.0, 0.0).astype(BF16), named.astype(BF16), ((1,), (0,)))
    rank = jnp.where(named > 0.0, rank, float(CAP)).astype(BF16)
    rows = experts * CAP
    spread = lax.broadcasted_iota(jnp.int32, (experts, rows), 0)
    spread = spread == lax.broadcasted_iota(jnp.int32, (experts, rows), 1) // CAP
    rank = dot(rank, jnp.where(spread, 1.0, 0.0).astype(BF16), ((1,), (0,)))
    row = lax.broadcasted_iota(jnp.int32, (tokens, rows), 1)
    slot = lax.rem(row, HELD).astype(F32)
    low = lax.rem(row, CAP) < HELD
    for core in range(CORES):
        hit = rank == slot + float(core * HELD)
        columns = slice(core * rows, (core + 1) * rows)
        mask_ref[:tokens, columns] = jnp.where(hit & low, 1.0, 0.0).astype(BF16)
        mask_ref[tokens:, columns] = jnp.where(hit & ~low, 1.0, 0.0).astype(BF16)


def gate_pick_body(core_ref, gate_ref, out_ref):
    rows = gate_ref[...].astype(F32).reshape(-1, 2, CAP, gate_ref.shape[1])
    even, odd = rows[:, 0], rows[:, 1]
    first, last = pack(even, odd, 0), pack(even, odd, 1)
    chosen = jnp.where(core_ref[0] == 0, first, last)
    out_ref[...] = chosen.reshape(out_ref.shape).astype(BF16)


def hidden_body(
    core_ref, rows_ref, mine_in, other_in, up_mine_in, up_other_in, keep_ref, send_ref, up_ref, w_ref, sems
):
    half = rows_ref.shape[-1]
    pieces = [(weight, side) for weight in (mine_in, other_in) for side in range(2)]
    loads = [
        pltpu.make_async_copy(weight.at[:, pl.ds(side * half, half)], w_ref.at[index], sems.at[index])
        for index, (weight, side) in enumerate(pieces)
    ]
    ups = [
        pltpu.make_async_copy(source, up_ref.at[index], sems.at[len(loads) + index])
        for index, source in enumerate((up_mine_in, up_other_in))
    ]
    loads[0].start()
    loads[1].start()
    parts = []
    for lane in (core_ref[0], 1 - core_ref[0]):
        rows = rows_ref[lane].astype(F32).reshape(-1, 2, CAP, half)
        for side in range(2):
            parts.append(pack(rows[:, 0], rows[:, 1], side).reshape(-1, half).astype(BF16))
    total = None
    for index, part in enumerate(parts):
        loads[index].wait()
        if index + 2 < len(loads):
            loads[index + 2].start()
        else:
            ups[index + 2 - len(loads)].start()
        term = dot(part, w_ref[index])
        total = term if total is None else total + term
    keep_ref[...] = total
    send_ref[...] = total.astype(BF16)
    for up in ups:
        up.wait()


def slot_grad_body(core_ref, keep_ref, away_ref, gate_ref, w_ref, mask_in, out_ref, mask_ref, sem):
    load = pltpu.make_async_copy(mask_in, mask_ref, sem)
    load.start()
    hidden = keep_ref[...] + away_ref[1 - core_ref[1]].astype(F32)
    up = (hidden * gate_ref[...].astype(F32)).astype(BF16)
    half = out_ref.shape[-1]
    for index, lane in enumerate((core_ref[0], 1 - core_ref[0])):
        left = dot(up, w_ref[index, :half, :]).reshape(-1, CAP, half)
        right = dot(up, w_ref[index, half:, :]).reshape(-1, CAP, half)
        out_ref[lane, :, 0] = pack(left, right, 0).astype(BF16)
        out_ref[lane, :, 1] = pack(left, right, 1).astype(BF16)
    load.wait()


def combine_body(mask_ref, back_ref, out_ref):
    tokens, half = out_ref.shape[0], back_ref.shape[1]
    both = dot(mask_ref[...], back_ref[...], ((1,), (0,))).astype(BF16)
    out_ref[:, :half] = both[:tokens]
    out_ref[:, half:] = both[tokens:]


def dense_part_body(core_ref, rows_ref, w_ref, mine_ref, other_ref, full_ref):
    half = mine_ref.shape[0]
    full_ref[...] = dot(rows_ref[...], w_ref[...])
    mine_ref[...] = full_ref[pl.ds(pl.multiple_of(core_ref[0] * half, 16), half), :]
    other_ref[...] = full_ref[pl.ds(pl.multiple_of((1 - core_ref[0]) * half, 16), half), :]


def dense_gate_body(core_ref, mine_ref, pair_ref, away_ref, gate_ref, up_ref):
    half = up_ref.shape[0]
    gate = gate_ref[pl.ds(pl.multiple_of(core_ref[0] * half, 16), half), :].astype(F32)
    hidden = mine_ref[...] + pair_ref[...] + away_ref[...].astype(F32)
    up_ref[...] = (hidden * gate).astype(BF16)


def dense_out_body(core_ref, mine_ref, other_ref, w_ref, out_ref):
    half = mine_ref.shape[0]
    grad = dot(jnp.concatenate([mine_ref[...], other_ref[...]], axis=0), w_ref[...]).astype(BF16)
    out_ref[pl.ds(pl.multiple_of(core_ref[0] * half, 16), half), :] = grad[:half]
    out_ref[pl.ds(pl.multiple_of((1 - core_ref[0]) * half, 16), half), :] = grad[half:]


def dense_up_grad(core, grad_out, shared_down, shared_gate):
    tokens, depth = grad_out.shape
    width = shared_down.shape[0]
    half = jax.ShapeDtypeStruct((tokens // 2, width), F32)
    mine, other = call(
        dense_part_body,
        (half, half),
        [SCALAR, WHOLE, WHOLE],
        [pltpu.VMEM((tokens, width), F32)],
        flops=2 * tokens * width * depth,
        moved=2 * width * depth,
    )(core, grad_out, shared_down)
    pair = lax.ppermute(other, "tensor", CORE_SWAP)
    away = lax.ppermute((mine + pair).astype(BF16), "tensor", CHIP_SWAP)
    up = call(
        dense_gate_body,
        jax.ShapeDtypeStruct((tokens // 2, width), BF16),
        [SCALAR] + [WHOLE] * 4,
        flops=3 * tokens * width,
        moved=7 * tokens * width,
    )(core, mine, pair, away, shared_gate)
    return up, lax.ppermute(up, "tensor", CORE_SWAP)


def on_device(
    grad_out, expert_ids, route_probs, saved_gate, w_up, w_down, shared_gate, shared_up, shared_down
):
    experts = lax.axis_size("expert")
    tokens, quarter = grad_out.shape
    half, slots, held = quarter // 2, experts * CAP, experts * HELD
    place = lax.axis_index("tensor")
    core = jnp.stack([place & 1, place >> 1])
    groups = [
        [place * 4 + chip * 2 + lane for lane in range(CORES) for place in range(experts)]
        for chip in range(2)
    ]

    def exchange(rows):
        rows = rows.reshape(CORES * experts, CAP, half)
        return lax.all_to_all(
            rows, ("expert", "tensor"), 0, 0, axis_index_groups=groups, tiled=True
        )

    ids, probs = expert_ids.T, route_probs.T
    sent = call(
        functools.partial(route_body, experts=experts),
        jax.ShapeDtypeStruct((CORES, experts // 2, 2, CAP, half), BF16),
        [FAR] * 3,
        [pltpu.VMEM(array.shape, array.dtype) for array in (ids, probs, grad_out)]
        + [
            pltpu.VMEM((CORES, experts // 2, 2, CAP, half), BF16),
            pltpu.SemaphoreType.DMA((3 + CORES,)),
        ],
        flops=2 * slots * tokens * quarter,
        moved=4 * slots * quarter,
        place=FAR,
    )(*far(ids, probs, grad_out))
    arrived = exchange(sent)

    down_other = lax.ppermute(w_down[0], "tensor", CORE_SWAP)
    up_other = lax.ppermute(w_up[0], "tensor", CORE_SWAP)
    width = w_down.shape[1]
    gate = call(
        gate_pick_body,
        jax.ShapeDtypeStruct((held, width), BF16),
        [SCALAR, WHOLE],
        flops=slots * width,
        moved=3 * slots * width,
    )(core, saved_gate[0, 0])
    dense_up = dense_up_grad(core, grad_out, shared_down, shared_gate)
    shared_grad = call(
        dense_out_body,
        jax.ShapeDtypeStruct((tokens, quarter), BF16),
        [SCALAR] + [WHOLE] * 3,
        flops=2 * tokens * quarter * shared_up.shape[1],
        moved=2 * quarter * shared_up.shape[1],
    )(core, *dense_up, shared_up)
    mask = call(
        functools.partial(mask_body, experts=experts),
        jax.ShapeDtypeStruct((2 * tokens, CORES * slots), BF16),
        [WHOLE],
        flops=2 * tokens * slots * experts,
        moved=4 * tokens * slots,
    )(expert_ids)
    arrived, down_other, up_other, gate, shared_grad, mask = lax.optimization_barrier(
        (arrived, down_other, up_other, gate, shared_grad, mask)
    )
    work = 4 * held * quarter * width
    keep, send, up_both = call(
        hidden_body,
        (
            jax.ShapeDtypeStruct(gate.shape, F32),
            jax.ShapeDtypeStruct(gate.shape, BF16),
            jax.ShapeDtypeStruct((CORES, quarter, width), BF16),
        ),
        [SCALAR, WHOLE] + [FAR] * 4,
        [pltpu.VMEM((2 * CORES, width, half), BF16), pltpu.SemaphoreType.DMA((3 * CORES,))],
        flops=work,
        moved=8 * quarter * width,
    )(
        core,
        arrived.reshape(CORES, experts, CAP, half),
        *far(w_down[0], down_other, w_up[0], up_other),
    )
    pair = [[lane, CORES + lane] for lane in range(CORES)]
    away = lax.all_gather(send, "tensor", axis_index_groups=pair)
    slot_grad, mask = call(
        slot_grad_body,
        (
            jax.ShapeDtypeStruct((CORES, experts // 2, 2, CAP, half), BF16),
            jax.ShapeDtypeStruct(mask.shape, BF16),
        ),
        [SCALAR] + [WHOLE] * 4 + [FAR],
        [pltpu.SemaphoreType.DMA(())],
        flops=work,
        moved=4 * quarter * width,
    )(core, keep, away, gate, up_both, *far(mask))
    back = exchange(slot_grad)
    moe_grad = call(
        combine_body,
        jax.ShapeDtypeStruct((tokens, quarter), BF16),
        [WHOLE] * 2,
        flops=4 * slots * tokens * quarter,
        moved=2 * slots * quarter,
    )(mask, back.reshape(CORES * slots, half))
    return (moe_grad, shared_grad)


def solution(mesh):
    placed = (
        P(("dp", "expert"), "tensor"),
        P(("dp", "expert"), None),
        P(("dp", "expert"), None),
        P("dp", "expert", None, None),
        P("expert", "tensor", None),
        P("expert", None, "tensor"),
        P(("dp", "expert"), None),
        P("tensor", None),
        P(None, "tensor"),
    )
    return jax.shard_map(
        on_device,
        mesh=mesh,
        in_specs=placed,
        out_specs=(P(("dp", "expert"), "tensor"), P(("dp", "expert"), "tensor")),
        check_vma=False,
    )
```

```python
import functools

import jax
import jax.numpy as jnp
from jax import lax
from jax.experimental import pallas as pl
from jax.experimental.pallas import tpu as pltpu
from jax.sharding import PartitionSpec as P

TOP = 6
CAP = 8
CORES = 2
CUTS = 2
HELD = CAP // CORES
CORE_SWAP = [(0, 1), (1, 0), (2, 3), (3, 2)]
CHIP_SWAP = [(0, 2), (1, 3), (2, 0), (3, 1)]
F32, BF16 = jnp.float32, jnp.bfloat16
WHOLE = pl.BlockSpec(memory_space=pltpu.VMEM)
FAR = pl.BlockSpec(memory_space=pltpu.HBM)
SCALAR = pl.BlockSpec(memory_space=pltpu.SMEM)


def dot(a, b, dims=((1,), (1,))):
    return lax.dot_general(a, b, (dims, ((), ())), preferred_element_type=F32)


def call(body, outs, specs, scratch=(), flops=0, moved=0, place=WHOLE):
    return pl.pallas_call(
        body,
        out_shape=outs,
        in_specs=specs,
        out_specs=jax.tree.map(lambda _: place, outs),
        scratch_shapes=list(scratch),
        compiler_params=pltpu.CompilerParams(vmem_limit_bytes=12 << 20),
        cost_estimate=pl.CostEstimate(flops=flops, bytes_accessed=moved, transcendentals=0),
    )


def far(*arrays):
    return tuple(pltpu.with_memory_space_constraint(array, pltpu.HBM) for array in arrays)


def low_rows(shape):
    return lax.broadcasted_iota(jnp.int32, shape, len(shape) - 2) < HELD


def pack(even, odd, side):
    low = low_rows(even.shape)
    if side == 0:
        return jnp.where(low, even, pltpu.roll(odd, HELD, 1))
    return jnp.where(low, pltpu.roll(even, HELD, 1), odd)


def route_body(
    ids_in, prob_in, grad_in, sent_out, ids_ref, prob_ref, grad_ref, sent_ref, sems, *, experts
):
    tokens, quarter = grad_ref.shape
    loads = [
        pltpu.make_async_copy(source, target, sems.at[index])
        for index, (source, target) in enumerate(
            ((ids_in, ids_ref), (prob_in, prob_ref), (grad_in, grad_ref))
        )
    ]
    for load in loads:
        load.start()
    loads[0].wait()
    loads[1].wait()
    pairs, half = experts // 2, quarter // 2
    row = lax.broadcasted_iota(jnp.int32, (experts, tokens), 0)
    expert = jnp.where(row < pairs, 2 * row, 2 * (row - pairs) + 1)
    named = jnp.zeros((experts, tokens), F32)
    prob = jnp.zeros((experts, tokens), F32)
    for pick in range(TOP):
        hit = ids_ref[pick : pick + 1, :] == expert
        named = jnp.where(hit, 1.0, named)
        prob = jnp.where(hit, prob_ref[pick : pick + 1, :], prob)
    square = (tokens, tokens)
    earlier = lax.broadcasted_iota(jnp.int32, square, 0) < lax.broadcasted_iota(jnp.int32, square, 1)
    rank = dot(named.astype(BF16), jnp.where(earlier, 1.0, 0.0).astype(BF16), ((1,), (0,)))
    rank = jnp.where(named > 0.0, rank, float(CAP))
    shape = (pairs, CAP, tokens)
    low = low_rows(shape)

    def spread(table):
        even = jnp.broadcast_to(table[:pairs, None, :], shape)
        return jnp.where(low, even, jnp.broadcast_to(table[pairs:, None, :], shape))

    rank, prob = spread(rank), spread(prob)
    slot = lax.rem(lax.broadcasted_iota(jnp.int32, shape, 1), HELD).astype(F32)
    loads[2].wait()
    stores = [
        pltpu.make_async_copy(sent_ref.at[core], sent_out.at[core], sems.at[3 + core])
        for core in range(CORES)
    ]
    for core in range(CORES):
        hit = rank == slot + float(core * HELD)
        scale = jnp.sum(jnp.where(hit, prob, 0.0), axis=2, keepdims=True)
        mask = jnp.where(hit, 1.0, 0.0).reshape(pairs * CAP, tokens).astype(BF16)
        left = dot(mask, grad_ref[:, :half], ((1,), (0,))).reshape(pairs, CAP, half) * scale
        right = dot(mask, grad_ref[:, half:], ((1,), (0,))).reshape(pairs, CAP, half) * scale
        sent_ref[core, :, 0] = pack(left, right, 0).astype(BF16)
        sent_ref[core, :, 1] = pack(left, right, 1).astype(BF16)
        stores[core].start()
    for store in stores:
        store.wait()


def prepare_body(
    ids_ref, keep_ref, away_ref, gate_ref, mine_in, other_in, up_ref, mask_ref, w_ref, sems, *, experts
):
    loads = [
        pltpu.make_async_copy(source, w_ref.at[index], sems.at[index])
        for index, source in enumerate((mine_in, other_in))
    ]
    for load in loads:
        load.start()
    hidden = keep_ref[...] + away_ref[...].astype(F32)
    up_ref[...] = (hidden * gate_ref[:, : up_ref.shape[1]].astype(F32)).astype(BF16)
    tokens = ids_ref.shape[0]
    expert = lax.broadcasted_iota(jnp.int32, (tokens, experts), 1)
    named = jnp.zeros((tokens, experts), F32)
    for pick in range(TOP):
        named = jnp.where(ids_ref[:, pick : pick + 1] == expert, 1.0, named)
    square = (tokens, tokens)
    earlier = lax.broadcasted_iota(jnp.int32, square, 1) < lax.broadcasted_iota(jnp.int32, square, 0)
    rank = dot(jnp.where(earlier, 1.0, 0.0).astype(BF16), named.astype(BF16), ((1,), (0,)))
    rank = jnp.where(named > 0.0, rank, float(CAP)).astype(BF16)
    rows = experts * CAP
    spread = lax.broadcasted_iota(jnp.int32, (experts, rows), 0)
    spread = spread == lax.broadcasted_iota(jnp.int32, (experts, rows), 1) // CAP
    rank = dot(rank, jnp.where(spread, 1.0, 0.0).astype(BF16), ((1,), (0,)))
    row = lax.broadcasted_iota(jnp.int32, (tokens, rows), 1)
    slot = lax.rem(row, HELD).astype(F32)
    low = lax.rem(row, CAP) < HELD
    for core in range(CORES):
        hit = rank == slot + float(core * HELD)
        columns = slice(core * rows, (core + 1) * rows)
        mask_ref[:tokens, columns] = jnp.where(hit & low, 1.0, 0.0).astype(BF16)
        mask_ref[tokens:, columns] = jnp.where(hit & ~low, 1.0, 0.0).astype(BF16)
    for load in loads:
        load.wait()


def gate_pick_body(core_ref, gate_ref, out_ref):
    rows = gate_ref[...].astype(F32).reshape(-1, 2, CAP, gate_ref.shape[1])
    even, odd = rows[:, 0], rows[:, 1]
    first, last = pack(even, odd, 0), pack(even, odd, 1)
    chosen = jnp.where(core_ref[0] == 0, first, last)
    out_ref[...] = chosen.reshape(out_ref.shape).astype(BF16)


def hidden_body(core_ref, rows_ref, mine_in, other_in, keep_ref, send_ref, w_ref, sems, *, first):
    count, half = keep_ref.shape[1], rows_ref.shape[-1]
    loads = [
        pltpu.make_async_copy(source.at[pl.ds(first, count), :], w_ref.at[index], sems.at[index])
        for index, source in enumerate((mine_in, other_in))
    ]
    for load in loads:
        load.start()
    parts = []
    for lane in (core_ref[0], 1 - core_ref[0]):
        rows = rows_ref[lane].astype(F32).reshape(-1, 2, CAP, half)
        for side in range(2):
            parts.append(pack(rows[:, 0], rows[:, 1], side).reshape(-1, half).astype(BF16))
    total = None
    for index, load in enumerate(loads):
        load.wait()
        for side in range(2):
            term = dot(parts[2 * index + side], w_ref[index, :, side * half : (side + 1) * half])
            total = term if total is None else total + term
    keep_ref[...] = total
    send_ref[...] = total.astype(BF16)


def slot_grad_body(core_ref, first_ref, keep_ref, away_ref, gate_ref, w_ref, out_ref):
    units, half = first_ref.shape[1], out_ref.shape[-1]
    hidden = keep_ref[...] + away_ref[...].astype(F32)
    last = (hidden * gate_ref[:, units:].astype(F32)).astype(BF16)
    up = jnp.concatenate([first_ref[...], last], axis=1)
    for index, lane in enumerate((core_ref[0], 1 - core_ref[0])):
        left = dot(up, w_ref[index, :half, :]).reshape(-1, CAP, half)
        right = dot(up, w_ref[index, half:, :]).reshape(-1, CAP, half)
        out_ref[lane, :, 0] = pack(left, right, 0).astype(BF16)
        out_ref[lane, :, 1] = pack(left, right, 1).astype(BF16)


def combine_body(mask_ref, back_ref, out_ref):
    tokens, half = out_ref.shape[0], back_ref.shape[1]
    both = dot(mask_ref[...], back_ref[...], ((1,), (0,))).astype(BF16)
    out_ref[:, :half] = both[:tokens]
    out_ref[:, half:] = both[tokens:]


def dense_part_body(core_ref, rows_ref, w_ref, mine_ref, other_ref, full_ref):
    half = mine_ref.shape[0]
    full_ref[...] = dot(rows_ref[...], w_ref[...])
    mine_ref[...] = full_ref[pl.ds(pl.multiple_of(core_ref[0] * half, 16), half), :]
    other_ref[...] = full_ref[pl.ds(pl.multiple_of((1 - core_ref[0]) * half, 16), half), :]


def dense_gate_body(core_ref, mine_ref, pair_ref, away_ref, gate_ref, up_ref):
    half = up_ref.shape[0]
    gate = gate_ref[pl.ds(pl.multiple_of(core_ref[0] * half, 16), half), :].astype(F32)
    hidden = mine_ref[...] + pair_ref[...] + away_ref[...].astype(F32)
    up_ref[...] = (hidden * gate).astype(BF16)


def dense_out_body(core_ref, mine_ref, other_ref, w_ref, out_ref):
    half = mine_ref.shape[0]
    grad = dot(jnp.concatenate([mine_ref[...], other_ref[...]], axis=0), w_ref[...]).astype(BF16)
    out_ref[pl.ds(pl.multiple_of(core_ref[0] * half, 16), half), :] = grad[:half]
    out_ref[pl.ds(pl.multiple_of((1 - core_ref[0]) * half, 16), half), :] = grad[half:]


def dense_up_grad(core, grad_out, shared_down, shared_gate):
    tokens, depth = grad_out.shape
    width = shared_down.shape[0]
    half = jax.ShapeDtypeStruct((tokens // 2, width), F32)
    mine, other = call(
        dense_part_body,
        (half, half),
        [SCALAR, WHOLE, WHOLE],
        [pltpu.VMEM((tokens, width), F32)],
        flops=2 * tokens * width * depth,
        moved=2 * width * depth,
    )(core, grad_out, shared_down)
    pair = lax.ppermute(other, "tensor", CORE_SWAP)
    away = lax.ppermute((mine + pair).astype(BF16), "tensor", CHIP_SWAP)
    up = call(
        dense_gate_body,
        jax.ShapeDtypeStruct((tokens // 2, width), BF16),
        [SCALAR] + [WHOLE] * 4,
        flops=3 * tokens * width,
        moved=7 * tokens * width,
    )(core, mine, pair, away, shared_gate)
    return up, lax.ppermute(up, "tensor", CORE_SWAP)


def on_device(
    grad_out, expert_ids, route_probs, saved_gate, w_up, w_down, shared_gate, shared_up, shared_down
):
    experts = lax.axis_size("expert")
    tokens, quarter = grad_out.shape
    half, slots, held = quarter // 2, experts * CAP, experts * HELD
    core = (lax.axis_index("tensor") & 1).reshape(1)
    groups = [
        [place * 4 + chip * 2 + lane for lane in range(CORES) for place in range(experts)]
        for chip in range(2)
    ]

    def exchange(rows):
        rows = rows.reshape(CORES * experts, CAP, half)
        return lax.all_to_all(
            rows, ("expert", "tensor"), 0, 0, axis_index_groups=groups, tiled=True
        )

    ids, probs = expert_ids.T, route_probs.T
    sent = call(
        functools.partial(route_body, experts=experts),
        jax.ShapeDtypeStruct((CORES, experts // 2, 2, CAP, half), BF16),
        [FAR] * 3,
        [pltpu.VMEM(array.shape, array.dtype) for array in (ids, probs, grad_out)]
        + [
            pltpu.VMEM((CORES, experts // 2, 2, CAP, half), BF16),
            pltpu.SemaphoreType.DMA((3 + CORES,)),
        ],
        flops=2 * slots * tokens * quarter,
        moved=4 * slots * quarter,
        place=FAR,
    )(*far(ids, probs, grad_out))
    arrived = exchange(sent)

    down_other = lax.ppermute(w_down[0], "tensor", CORE_SWAP)
    up_other = lax.ppermute(w_up[0], "tensor", CORE_SWAP)
    width = w_down.shape[1]
    gate = call(
        gate_pick_body,
        jax.ShapeDtypeStruct((held, width), BF16),
        [SCALAR, WHOLE],
        flops=slots * width,
        moved=3 * slots * width,
    )(core, saved_gate[0, 0])
    dense_up = dense_up_grad(core, grad_out, shared_down, shared_gate)
    shared_grad = call(
        dense_out_body,
        jax.ShapeDtypeStruct((tokens, quarter), BF16),
        [SCALAR] + [WHOLE] * 3,
        flops=2 * tokens * quarter * shared_up.shape[1],
        moved=2 * quarter * shared_up.shape[1],
    )(core, *dense_up, shared_up)
    ids, arrived, down_other, up_other, gate, shared_grad = lax.optimization_barrier(
        (expert_ids, arrived, down_other, up_other, gate, shared_grad)
    )
    work = 4 * held * quarter * width
    units = width // CUTS
    rows = arrived.reshape(CORES, experts, CAP, half)
    keeps, aways = [], []
    for cut in range(CUTS):
        keep, send = call(
            functools.partial(hidden_body, first=cut * units),
            (jax.ShapeDtypeStruct((held, units), F32), jax.ShapeDtypeStruct((held, units), BF16)),
            [SCALAR, WHOLE, FAR, FAR],
            [pltpu.VMEM((CORES, units, quarter), BF16), pltpu.SemaphoreType.DMA((CORES,))],
            flops=work // CUTS,
            moved=4 * quarter * units,
        )(core, rows, *far(w_down[0], down_other))
        keeps.append(keep)
        aways.append(lax.ppermute(send, "tensor", CHIP_SWAP))
    first, mask, w_both = call(
        functools.partial(prepare_body, experts=experts),
        (
            jax.ShapeDtypeStruct((held, units), BF16),
            jax.ShapeDtypeStruct((2 * tokens, CORES * slots), BF16),
            jax.ShapeDtypeStruct((CORES, quarter, width), BF16),
        ),
        [WHOLE] * 4 + [FAR] * 2,
        [pltpu.SemaphoreType.DMA((CORES,))],
        flops=2 * tokens * slots * experts,
        moved=4 * quarter * width,
    )(ids, keeps[0], aways[0], gate, *far(w_up[0], up_other))
    slot_grad = call(
        slot_grad_body,
        jax.ShapeDtypeStruct((CORES, experts // 2, 2, CAP, half), BF16),
        [SCALAR] + [WHOLE] * 5,
        flops=work,
        moved=4 * quarter * width,
    )(core, first, keeps[1], aways[1], gate, w_both)
    back = exchange(slot_grad)
    moe_grad = call(
        combine_body,
        jax.ShapeDtypeStruct((tokens, quarter), BF16),
        [WHOLE] * 2,
        flops=4 * slots * tokens * quarter,
        moved=2 * slots * quarter,
    )(mask, back.reshape(CORES * slots, half))
    return (moe_grad, shared_grad)


def solution(mesh):
    placed = (
        P(("dp", "expert"), "tensor"),
        P(("dp", "expert"), None),
        P(("dp", "expert"), None),
        P("dp", "expert", None, None),
        P("expert", "tensor", None),
        P("expert", None, "tensor"),
        P(("dp", "expert"), None),
        P("tensor", None),
        P(None, "tensor"),
    )
    return jax.shard_map(
        on_device,
        mesh=mesh,
        in_specs=placed,
        out_specs=(P(("dp", "expert"), "tensor"), P(("dp", "expert"), "tensor")),
        check_vma=False,
    )
```

```python
import functools

import jax
import jax.numpy as jnp
from jax import lax
from jax.experimental import pallas as pl
from jax.experimental.pallas import tpu as pltpu
from jax.sharding import PartitionSpec as P

TOP = 6
CAP = 8
CORES = 2
HELD = CAP // CORES
CORE_SWAP = [(0, 1), (1, 0), (2, 3), (3, 2)]
CHIP_SWAP = [(0, 2), (1, 3), (2, 0), (3, 1)]
F32, BF16 = jnp.float32, jnp.bfloat16
WHOLE = pl.BlockSpec(memory_space=pltpu.VMEM)
FAR = pl.BlockSpec(memory_space=pltpu.HBM)
ANY = pl.BlockSpec(memory_space=pl.ANY)
SCALAR = pl.BlockSpec(memory_space=pltpu.SMEM)


def dot(a, b, dims=((1,), (1,))):
    return lax.dot_general(a, b, (dims, ((), ())), preferred_element_type=F32)


def call(body, outs, specs, scratch=(), flops=0, moved=0, place=WHOLE):
    return pl.pallas_call(
        body,
        out_shape=outs,
        in_specs=specs,
        out_specs=jax.tree.map(lambda _: place, outs),
        scratch_shapes=list(scratch),
        compiler_params=pltpu.CompilerParams(vmem_limit_bytes=12 << 20),
        cost_estimate=pl.CostEstimate(flops=flops, bytes_accessed=moved, transcendentals=0),
    )


def far(*arrays):
    return tuple(pltpu.with_memory_space_constraint(array, pltpu.HBM) for array in arrays)


def low_rows(shape):
    return lax.broadcasted_iota(jnp.int32, shape, len(shape) - 2) < HELD


def pack(even, odd, side):
    low = low_rows(even.shape)
    if side == 0:
        return jnp.where(low, even, pltpu.roll(odd, HELD, 1))
    return jnp.where(low, pltpu.roll(even, HELD, 1), odd)


def route_body(
    ids_in, prob_in, grad_in, sent_out, ids_ref, prob_ref, grad_ref, sent_ref, sems, *, experts
):
    tokens, quarter = grad_ref.shape
    loads = [
        pltpu.make_async_copy(source, target, sems.at[index])
        for index, (source, target) in enumerate(
            ((ids_in, ids_ref), (prob_in, prob_ref), (grad_in, grad_ref))
        )
    ]
    for load in loads:
        load.start()
    loads[0].wait()
    loads[1].wait()
    pairs, half = experts // 2, quarter // 2
    row = lax.broadcasted_iota(jnp.int32, (experts, tokens), 0)
    expert = jnp.where(row < pairs, 2 * row, 2 * (row - pairs) + 1)
    named = jnp.zeros((experts, tokens), F32)
    prob = jnp.zeros((experts, tokens), F32)
    for pick in range(TOP):
        hit = ids_ref[pick : pick + 1, :] == expert
        named = jnp.where(hit, 1.0, named)
        prob = jnp.where(hit, prob_ref[pick : pick + 1, :], prob)
    square = (tokens, tokens)
    earlier = lax.broadcasted_iota(jnp.int32, square, 0) < lax.broadcasted_iota(jnp.int32, square, 1)
    rank = dot(named.astype(BF16), jnp.where(earlier, 1.0, 0.0).astype(BF16), ((1,), (0,)))
    rank = jnp.where(named > 0.0, rank, float(CAP))
    shape = (pairs, CAP, tokens)
    low = low_rows(shape)

    def spread(table):
        even = jnp.broadcast_to(table[:pairs, None, :], shape)
        return jnp.where(low, even, jnp.broadcast_to(table[pairs:, None, :], shape))

    rank, prob = spread(rank), spread(prob)
    slot = lax.rem(lax.broadcasted_iota(jnp.int32, shape, 1), HELD).astype(F32)
    loads[2].wait()
    stores = [
        pltpu.make_async_copy(sent_ref.at[core], sent_out.at[core], sems.at[3 + core])
        for core in range(CORES)
    ]
    for core in range(CORES):
        hit = rank == slot + float(core * HELD)
        scale = jnp.sum(jnp.where(hit, prob, 0.0), axis=2, keepdims=True)
        mask = jnp.where(hit, 1.0, 0.0).reshape(pairs * CAP, tokens).astype(BF16)
        left = dot(mask, grad_ref[:, :half], ((1,), (0,))).reshape(pairs, CAP, half) * scale
        right = dot(mask, grad_ref[:, half:], ((1,), (0,))).reshape(pairs, CAP, half) * scale
        sent_ref[core, :, 0] = pack(left, right, 0).astype(BF16)
        sent_ref[core, :, 1] = pack(left, right, 1).astype(BF16)
        stores[core].start()
    for store in stores:
        store.wait()


def prepare_body(
    ids_ref, own_in, mine_in, other_in, mask_ref, w_ref, own_ref, sems, *, experts
):
    loads = [
        pltpu.make_async_copy(source, w_ref.at[index], sems.at[index])
        for index, source in enumerate((mine_in, other_in))
    ]
    loads.append(pltpu.make_async_copy(own_in, own_ref, sems.at[CORES]))
    for load in loads:
        load.start()
    tokens = ids_ref.shape[0]
    expert = lax.broadcasted_iota(jnp.int32, (tokens, experts), 1)
    named = jnp.zeros((tokens, experts), F32)
    for pick in range(TOP):
        named = jnp.where(ids_ref[:, pick : pick + 1] == expert, 1.0, named)
    square = (tokens, tokens)
    earlier = lax.broadcasted_iota(jnp.int32, square, 1) < lax.broadcasted_iota(jnp.int32, square, 0)
    rank = dot(jnp.where(earlier, 1.0, 0.0).astype(BF16), named.astype(BF16), ((1,), (0,)))
    rank = jnp.where(named > 0.0, rank, float(CAP)).astype(BF16)
    rows = experts * CAP
    spread = lax.broadcasted_iota(jnp.int32, (experts, rows), 0)
    spread = spread == lax.broadcasted_iota(jnp.int32, (experts, rows), 1) // CAP
    rank = dot(rank, jnp.where(spread, 1.0, 0.0).astype(BF16), ((1,), (0,)))
    row = lax.broadcasted_iota(jnp.int32, (tokens, rows), 1)
    slot = lax.rem(row, HELD).astype(F32)
    low = lax.rem(row, CAP) < HELD
    for core in range(CORES):
        hit = rank == slot + float(core * HELD)
        columns = slice(core * rows, (core + 1) * rows)
        mask_ref[:tokens, columns] = jnp.where(hit & low, 1.0, 0.0).astype(BF16)
        mask_ref[tokens:, columns] = jnp.where(hit & ~low, 1.0, 0.0).astype(BF16)
    for load in loads:
        load.wait()


def gate_pick_body(core_ref, gate_ref, out_ref):
    rows = gate_ref[...].astype(F32).reshape(-1, 2, CAP, gate_ref.shape[1])
    even, odd = rows[:, 0], rows[:, 1]
    first, last = pack(even, odd, 0), pack(even, odd, 1)
    chosen = jnp.where(core_ref[0] == 0, first, last)
    out_ref[...] = chosen.reshape(out_ref.shape).astype(BF16)


def bring_body(source_in, after_in, near_ref, sem):
    load = pltpu.make_async_copy(source_in, near_ref, sem)
    load.start()
    load.wait()


def hidden_body(core_ref, rows_ref, mine_in, other_ref, send_ref, w_ref, sems):
    half = rows_ref.shape[-1]
    loads = [
        pltpu.make_async_copy(mine_in.at[:, pl.ds(side * half, half)], w_ref.at[side], sems.at[side])
        for side in range(2)
    ]
    for load in loads:
        load.start()
    parts = []
    for lane in (1 - core_ref[0], core_ref[0]):
        rows = rows_ref[lane].astype(F32).reshape(-1, 2, CAP, half)
        for side in range(2):
            parts.append(pack(rows[:, 0], rows[:, 1], side).reshape(-1, half).astype(BF16))
    total = dot(parts[0], other_ref[:, :half]) + dot(parts[1], other_ref[:, half:])
    for side, load in enumerate(loads):
        load.wait()
        total = total + dot(parts[2 + side], w_ref[side])
    send_ref[...] = total.astype(BF16)


def slot_grad_body(core_ref, own_ref, away_ref, gate_ref, w_ref, mask_in, out_ref):
    hidden = own_ref[...].astype(F32) + away_ref[...].astype(F32)
    up = (hidden * gate_ref[...].astype(F32)).astype(BF16)
    half = out_ref.shape[-1]
    for index, lane in enumerate((core_ref[0], 1 - core_ref[0])):
        left = dot(up, w_ref[index, :half, :]).reshape(-1, CAP, half)
        right = dot(up, w_ref[index, half:, :]).reshape(-1, CAP, half)
        out_ref[lane, :, 0] = pack(left, right, 0).astype(BF16)
        out_ref[lane, :, 1] = pack(left, right, 1).astype(BF16)


def combine_body(mask_ref, back_ref, out_ref):
    tokens, half = out_ref.shape[0], back_ref.shape[1]
    both = dot(mask_ref[...], back_ref[...], ((1,), (0,))).astype(BF16)
    out_ref[:, :half] = both[:tokens]
    out_ref[:, half:] = both[tokens:]


def dense_part_body(core_ref, rows_ref, w_ref, mine_ref, other_ref, full_ref):
    half = mine_ref.shape[0]
    full_ref[...] = dot(rows_ref[...], w_ref[...])
    mine_ref[...] = full_ref[pl.ds(pl.multiple_of(core_ref[0] * half, 16), half), :]
    other_ref[...] = full_ref[pl.ds(pl.multiple_of((1 - core_ref[0]) * half, 16), half), :]


def dense_gate_body(core_ref, mine_ref, pair_ref, away_ref, gate_ref, up_ref):
    half = up_ref.shape[0]
    gate = gate_ref[pl.ds(pl.multiple_of(core_ref[0] * half, 16), half), :].astype(F32)
    hidden = mine_ref[...] + pair_ref[...] + away_ref[...].astype(F32)
    up_ref[...] = (hidden * gate).astype(BF16)


def dense_out_body(core_ref, mine_ref, other_ref, w_ref, out_ref):
    half = mine_ref.shape[0]
    grad = dot(jnp.concatenate([mine_ref[...], other_ref[...]], axis=0), w_ref[...]).astype(BF16)
    out_ref[pl.ds(pl.multiple_of(core_ref[0] * half, 16), half), :] = grad[:half]
    out_ref[pl.ds(pl.multiple_of((1 - core_ref[0]) * half, 16), half), :] = grad[half:]


def dense_up_grad(core, grad_out, shared_down, shared_gate):
    tokens, depth = grad_out.shape
    width = shared_down.shape[0]
    half = jax.ShapeDtypeStruct((tokens // 2, width), F32)
    mine, other = call(
        dense_part_body,
        (half, half),
        [SCALAR, WHOLE, WHOLE],
        [pltpu.VMEM((tokens, width), F32)],
        flops=2 * tokens * width * depth,
        moved=2 * width * depth,
    )(core, grad_out, shared_down)
    pair = lax.ppermute(other, "tensor", CORE_SWAP)
    away = lax.ppermute((mine + pair).astype(BF16), "tensor", CHIP_SWAP)
    up = call(
        dense_gate_body,
        jax.ShapeDtypeStruct((tokens // 2, width), BF16),
        [SCALAR] + [WHOLE] * 4,
        flops=3 * tokens * width,
        moved=7 * tokens * width,
    )(core, mine, pair, away, shared_gate)
    return up, lax.ppermute(up, "tensor", CORE_SWAP)


def on_device(
    grad_out, expert_ids, route_probs, saved_gate, w_up, w_down, shared_gate, shared_up, shared_down
):
    experts = lax.axis_size("expert")
    tokens, quarter = grad_out.shape
    half, slots, held = quarter // 2, experts * CAP, experts * HELD
    core = (lax.axis_index("tensor") & 1).reshape(1)
    groups = [
        [place * 4 + chip * 2 + lane for lane in range(CORES) for place in range(experts)]
        for chip in range(2)
    ]

    def exchange(rows):
        rows = rows.reshape(CORES * experts, CAP, half)
        return lax.all_to_all(
            rows, ("expert", "tensor"), 0, 0, axis_index_groups=groups, tiled=True
        )

    ids, probs = expert_ids.T, route_probs.T
    sent = call(
        functools.partial(route_body, experts=experts),
        jax.ShapeDtypeStruct((CORES, experts // 2, 2, CAP, half), BF16),
        [FAR] * 3,
        [pltpu.VMEM(array.shape, array.dtype) for array in (ids, probs, grad_out)]
        + [
            pltpu.VMEM((CORES, experts // 2, 2, CAP, half), BF16),
            pltpu.SemaphoreType.DMA((3 + CORES,)),
        ],
        flops=2 * slots * tokens * quarter,
        moved=4 * slots * quarter,
        place=FAR,
    )(*far(ids, probs, grad_out))
    arrived = exchange(sent)

    down_other = lax.ppermute(w_down[0], "tensor", CORE_SWAP)
    up_other = lax.ppermute(w_up[0], "tensor", CORE_SWAP)
    width = w_down.shape[1]
    gate = call(
        gate_pick_body,
        jax.ShapeDtypeStruct((held, width), BF16),
        [SCALAR, WHOLE],
        flops=slots * width,
        moved=3 * slots * width,
    )(core, saved_gate[0, 0])
    dense_up = dense_up_grad(core, grad_out, shared_down, shared_gate)
    shared_grad = call(
        dense_out_body,
        jax.ShapeDtypeStruct((tokens, quarter), BF16),
        [SCALAR] + [WHOLE] * 3,
        flops=2 * tokens * quarter * shared_up.shape[1],
        moved=2 * quarter * shared_up.shape[1],
    )(core, *dense_up, shared_up)
    down_other = call(
        bring_body,
        jax.ShapeDtypeStruct(down_other.shape, BF16),
        [FAR, ANY],
        [pltpu.SemaphoreType.DMA(())],
        moved=4 * quarter * width,
    )(*far(down_other), shared_grad)
    ids, arrived, down_other, up_other, gate, shared_grad = lax.optimization_barrier(
        (expert_ids, arrived, down_other, up_other, gate, shared_grad)
    )
    work = 4 * held * quarter * width
    send = call(
        hidden_body,
        jax.ShapeDtypeStruct(gate.shape, BF16),
        [SCALAR, WHOLE, FAR, WHOLE],
        [pltpu.VMEM((2, width, half), BF16), pltpu.SemaphoreType.DMA((2,))],
        flops=work,
        moved=4 * quarter * width,
    )(core, arrived.reshape(CORES, experts, CAP, half), *far(w_down[0]), down_other)
    away = lax.ppermute(send, "tensor", CHIP_SWAP)
    mask, w_both, own = call(
        functools.partial(prepare_body, experts=experts),
        (
            jax.ShapeDtypeStruct((2 * tokens, CORES * slots), BF16),
            jax.ShapeDtypeStruct((CORES, quarter, width), BF16),
            jax.ShapeDtypeStruct(gate.shape, BF16),
        ),
        [WHOLE] + [FAR] * 3,
        [pltpu.SemaphoreType.DMA((CORES + 1,))],
        flops=2 * tokens * slots * experts,
        moved=4 * quarter * width,
    )(ids, *far(send, w_up[0], up_other))
    slot_grad = call(
        slot_grad_body,
        jax.ShapeDtypeStruct((CORES, experts // 2, 2, CAP, half), BF16),
        [SCALAR] + [WHOLE] * 4 + [ANY],
        flops=work,
        moved=4 * quarter * width,
    )(core, own, away, gate, w_both, mask)
    back = exchange(slot_grad)
    moe_grad = call(
        combine_body,
        jax.ShapeDtypeStruct((tokens, quarter), BF16),
        [WHOLE] * 2,
        flops=4 * slots * tokens * quarter,
        moved=2 * slots * quarter,
    )(mask, back.reshape(CORES * slots, half))
    return (moe_grad, shared_grad)


def solution(mesh):
    placed = (
        P(("dp", "expert"), "tensor"),
        P(("dp", "expert"), None),
        P(("dp", "expert"), None),
        P("dp", "expert", None, None),
        P("expert", "tensor", None),
        P("expert", None, "tensor"),
        P(("dp", "expert"), None),
        P("tensor", None),
        P(None, "tensor"),
    )
    return jax.shard_map(
        on_device,
        mesh=mesh,
        in_specs=placed,
        out_specs=(P(("dp", "expert"), "tensor"), P(("dp", "expert"), "tensor")),
        check_vma=False,
    )
```

```python
import functools

import jax
import jax.numpy as jnp
from jax import lax
from jax.experimental import pallas as pl
from jax.experimental.pallas import tpu as pltpu
from jax.sharding import PartitionSpec as P

TOP = 6
CAP = 8
CORES = 2
HELD = CAP // CORES
CORE_SWAP = [(0, 1), (1, 0), (2, 3), (3, 2)]
CHIP_SWAP = [(0, 2), (1, 3), (2, 0), (3, 1)]
F32, BF16 = jnp.float32, jnp.bfloat16
WHOLE = pl.BlockSpec(memory_space=pltpu.VMEM)
FAR = pl.BlockSpec(memory_space=pltpu.HBM)
ANY = pl.BlockSpec(memory_space=pl.ANY)
SCALAR = pl.BlockSpec(memory_space=pltpu.SMEM)


def dot(a, b, dims=((1,), (1,))):
    return lax.dot_general(a, b, (dims, ((), ())), preferred_element_type=F32)


def call(body, outs, specs, scratch=(), flops=0, moved=0, place=WHOLE):
    return pl.pallas_call(
        body,
        out_shape=outs,
        in_specs=specs,
        out_specs=jax.tree.map(lambda _: place, outs),
        scratch_shapes=list(scratch),
        compiler_params=pltpu.CompilerParams(vmem_limit_bytes=12 << 20),
        cost_estimate=pl.CostEstimate(flops=flops, bytes_accessed=moved, transcendentals=0),
    )


def far(*arrays):
    return tuple(pltpu.with_memory_space_constraint(array, pltpu.HBM) for array in arrays)


def low_rows(shape):
    return lax.broadcasted_iota(jnp.int32, shape, len(shape) - 2) < HELD


def pack(even, odd, side):
    low = low_rows(even.shape)
    if side == 0:
        return jnp.where(low, even, pltpu.roll(odd, HELD, 1))
    return jnp.where(low, pltpu.roll(even, HELD, 1), odd)


def route_body(
    ids_in, prob_in, grad_in, sent_out, ids_ref, prob_ref, grad_ref, sent_ref, sems, *, experts
):
    tokens, quarter = grad_ref.shape
    loads = [
        pltpu.make_async_copy(source, target, sems.at[index])
        for index, (source, target) in enumerate(
            ((ids_in, ids_ref), (prob_in, prob_ref), (grad_in, grad_ref))
        )
    ]
    for load in loads:
        load.start()
    loads[0].wait()
    loads[1].wait()
    pairs, half = experts // 2, quarter // 2
    row = lax.broadcasted_iota(jnp.int32, (experts, tokens), 0)
    expert = jnp.where(row < pairs, 2 * row, 2 * (row - pairs) + 1)
    named = jnp.zeros((experts, tokens), F32)
    prob = jnp.zeros((experts, tokens), F32)
    for pick in range(TOP):
        hit = ids_ref[pick : pick + 1, :] == expert
        named = jnp.where(hit, 1.0, named)
        prob = jnp.where(hit, prob_ref[pick : pick + 1, :], prob)
    square = (tokens, tokens)
    earlier = lax.broadcasted_iota(jnp.int32, square, 0) < lax.broadcasted_iota(jnp.int32, square, 1)
    rank = dot(named.astype(BF16), jnp.where(earlier, 1.0, 0.0).astype(BF16), ((1,), (0,)))
    rank = jnp.where(named > 0.0, rank, float(CAP))
    shape = (pairs, CAP, tokens)
    low = low_rows(shape)

    def spread(table):
        even = jnp.broadcast_to(table[:pairs, None, :], shape)
        return jnp.where(low, even, jnp.broadcast_to(table[pairs:, None, :], shape))

    rank, prob = spread(rank), spread(prob)
    slot = lax.rem(lax.broadcasted_iota(jnp.int32, shape, 1), HELD).astype(F32)
    loads[2].wait()
    stores = [
        pltpu.make_async_copy(sent_ref.at[core], sent_out.at[core], sems.at[3 + core])
        for core in range(CORES)
    ]
    for core in range(CORES):
        hit = rank == slot + float(core * HELD)
        scale = jnp.sum(jnp.where(hit, prob, 0.0), axis=2, keepdims=True)
        mask = jnp.where(hit, 1.0, 0.0).reshape(pairs * CAP, tokens).astype(BF16)
        left = dot(mask, grad_ref[:, :half], ((1,), (0,))).reshape(pairs, CAP, half) * scale
        right = dot(mask, grad_ref[:, half:], ((1,), (0,))).reshape(pairs, CAP, half) * scale
        sent_ref[core, :, 0] = pack(left, right, 0).astype(BF16)
        sent_ref[core, :, 1] = pack(left, right, 1).astype(BF16)
        stores[core].start()
    for store in stores:
        store.wait()


def prepare_body(ids_ref, after_ref, mine_in, other_in, mask_ref, w_ref, sems, *, experts):
    loads = [
        pltpu.make_async_copy(source, w_ref.at[index], sems.at[index])
        for index, source in enumerate((mine_in, other_in))
    ]
    for load in loads:
        load.start()
    tokens = ids_ref.shape[0]
    expert = lax.broadcasted_iota(jnp.int32, (tokens, experts), 1)
    named = jnp.zeros((tokens, experts), F32)
    for pick in range(TOP):
        named = jnp.where(ids_ref[:, pick : pick + 1] == expert, 1.0, named)
    square = (tokens, tokens)
    earlier = lax.broadcasted_iota(jnp.int32, square, 1) < lax.broadcasted_iota(jnp.int32, square, 0)
    rank = dot(jnp.where(earlier, 1.0, 0.0).astype(BF16), named.astype(BF16), ((1,), (0,)))
    rank = jnp.where(named > 0.0, rank, float(CAP)).astype(BF16)
    rows = experts * CAP
    spread = lax.broadcasted_iota(jnp.int32, (experts, rows), 0)
    spread = spread == lax.broadcasted_iota(jnp.int32, (experts, rows), 1) // CAP
    rank = dot(rank, jnp.where(spread, 1.0, 0.0).astype(BF16), ((1,), (0,)))
    row = lax.broadcasted_iota(jnp.int32, (tokens, rows), 1)
    slot = lax.rem(row, HELD).astype(F32)
    low = lax.rem(row, CAP) < HELD
    for core in range(CORES):
        hit = rank == slot + float(core * HELD)
        columns = slice(core * rows, (core + 1) * rows)
        mask_ref[:tokens, columns] = jnp.where(hit & low, 1.0, 0.0).astype(BF16)
        mask_ref[tokens:, columns] = jnp.where(hit & ~low, 1.0, 0.0).astype(BF16)
    for load in loads:
        load.wait()


def gate_pick_body(core_ref, gate_ref, out_ref):
    rows = gate_ref[...].astype(F32).reshape(-1, 2, CAP, gate_ref.shape[1])
    even, odd = rows[:, 0], rows[:, 1]
    first, last = pack(even, odd, 0), pack(even, odd, 1)
    chosen = jnp.where(core_ref[0] == 0, first, last)
    out_ref[...] = chosen.reshape(out_ref.shape).astype(BF16)


def hidden_body(core_ref, rows_ref, mine_in, other_in, keep_ref, send_ref, w_ref, sems):
    loads = [
        pltpu.make_async_copy(source, w_ref.at[index], sems.at[index])
        for index, source in enumerate((mine_in, other_in))
    ]
    for load in loads:
        load.start()
    total = None
    for index, lane in enumerate((core_ref[0], 1 - core_ref[0])):
        rows = rows_ref[lane].astype(F32)
        half = rows.shape[-1]
        rows = rows.reshape(-1, 2, CAP, half)
        parts = [pack(rows[:, 0], rows[:, 1], side).reshape(-1, half).astype(BF16) for side in range(2)]
        loads[index].wait()
        for side, part in enumerate(parts):
            term = dot(part, w_ref[index, :, side * half : (side + 1) * half])
            total = term if total is None else total + term
    keep_ref[...] = total
    send_ref[...] = total.astype(BF16)


def slot_grad_body(core_ref, keep_ref, away_ref, gate_ref, w_ref, mask_in, out_ref):
    hidden = keep_ref[...] + away_ref[...].astype(F32)
    up = (hidden * gate_ref[...].astype(F32)).astype(BF16)
    half = out_ref.shape[-1]
    for index, lane in enumerate((core_ref[0], 1 - core_ref[0])):
        left = dot(up, w_ref[index, :half, :]).reshape(-1, CAP, half)
        right = dot(up, w_ref[index, half:, :]).reshape(-1, CAP, half)
        out_ref[lane, :, 0] = pack(left, right, 0).astype(BF16)
        out_ref[lane, :, 1] = pack(left, right, 1).astype(BF16)


def combine_body(mask_ref, back_ref, out_ref):
    tokens, half = out_ref.shape[0], back_ref.shape[1]
    both = dot(mask_ref[...], back_ref[...], ((1,), (0,))).astype(BF16)
    out_ref[:, :half] = both[:tokens]
    out_ref[:, half:] = both[tokens:]


def dense_part_body(core_ref, rows_ref, w_ref, mine_ref, other_ref, full_ref):
    half = mine_ref.shape[0]
    full_ref[...] = dot(rows_ref[...], w_ref[...])
    mine_ref[...] = full_ref[pl.ds(pl.multiple_of(core_ref[0] * half, 16), half), :]
    other_ref[...] = full_ref[pl.ds(pl.multiple_of((1 - core_ref[0]) * half, 16), half), :]


def dense_gate_body(core_ref, mine_ref, pair_ref, away_ref, gate_ref, up_ref):
    half = up_ref.shape[0]
    gate = gate_ref[pl.ds(pl.multiple_of(core_ref[0] * half, 16), half), :].astype(F32)
    hidden = mine_ref[...] + pair_ref[...] + away_ref[...].astype(F32)
    up_ref[...] = (hidden * gate).astype(BF16)


def dense_out_body(core_ref, mine_ref, other_ref, w_ref, out_ref):
    half = mine_ref.shape[0]
    grad = dot(jnp.concatenate([mine_ref[...], other_ref[...]], axis=0), w_ref[...]).astype(BF16)
    out_ref[pl.ds(pl.multiple_of(core_ref[0] * half, 16), half), :] = grad[:half]
    out_ref[pl.ds(pl.multiple_of((1 - core_ref[0]) * half, 16), half), :] = grad[half:]


def dense_up_grad(core, grad_out, shared_down, shared_gate):
    tokens, depth = grad_out.shape
    width = shared_down.shape[0]
    half = jax.ShapeDtypeStruct((tokens // 2, width), F32)
    mine, other = call(
        dense_part_body,
        (half, half),
        [SCALAR, WHOLE, WHOLE],
        [pltpu.VMEM((tokens, width), F32)],
        flops=2 * tokens * width * depth,
        moved=2 * width * depth,
    )(core, grad_out, shared_down)
    pair = lax.ppermute(other, "tensor", CORE_SWAP)
    away = lax.ppermute((mine + pair).astype(BF16), "tensor", CHIP_SWAP)
    up = call(
        dense_gate_body,
        jax.ShapeDtypeStruct((tokens // 2, width), BF16),
        [SCALAR] + [WHOLE] * 4,
        flops=3 * tokens * width,
        moved=7 * tokens * width,
    )(core, mine, pair, away, shared_gate)
    return up, lax.ppermute(up, "tensor", CORE_SWAP)


def on_device(
    grad_out, expert_ids, route_probs, saved_gate, w_up, w_down, shared_gate, shared_up, shared_down
):
    experts = lax.axis_size("expert")
    tokens, quarter = grad_out.shape
    half, slots, held = quarter // 2, experts * CAP, experts * HELD
    core = (lax.axis_index("tensor") & 1).reshape(1)
    groups = [
        [place * 4 + chip * 2 + lane for lane in range(CORES) for place in range(experts)]
        for chip in range(2)
    ]

    def exchange(rows):
        rows = rows.reshape(CORES * experts, CAP, half)
        return lax.all_to_all(
            rows, ("expert", "tensor"), 0, 0, axis_index_groups=groups, tiled=True
        )

    ids, probs = expert_ids.T, route_probs.T
    sent = call(
        functools.partial(route_body, experts=experts),
        jax.ShapeDtypeStruct((CORES, experts // 2, 2, CAP, half), BF16),
        [FAR] * 3,
        [pltpu.VMEM(array.shape, array.dtype) for array in (ids, probs, grad_out)]
        + [
            pltpu.VMEM((CORES, experts // 2, 2, CAP, half), BF16),
            pltpu.SemaphoreType.DMA((3 + CORES,)),
        ],
        flops=2 * slots * tokens * quarter,
        moved=4 * slots * quarter,
        place=FAR,
    )(*far(ids, probs, grad_out))
    arrived = exchange(sent)

    down_other = lax.ppermute(w_down[0], "tensor", CORE_SWAP)
    up_other = lax.ppermute(w_up[0], "tensor", CORE_SWAP)
    width = w_down.shape[1]
    gate = call(
        gate_pick_body,
        jax.ShapeDtypeStruct((held, width), BF16),
        [SCALAR, WHOLE],
        flops=slots * width,
        moved=3 * slots * width,
    )(core, saved_gate[0, 0])
    dense_up = dense_up_grad(core, grad_out, shared_down, shared_gate)
    shared_grad = call(
        dense_out_body,
        jax.ShapeDtypeStruct((tokens, quarter), BF16),
        [SCALAR] + [WHOLE] * 3,
        flops=2 * tokens * quarter * shared_up.shape[1],
        moved=2 * quarter * shared_up.shape[1],
    )(core, *dense_up, shared_up)
    ids, arrived, down_other, up_other, gate, shared_grad = lax.optimization_barrier(
        (expert_ids, arrived, down_other, up_other, gate, shared_grad)
    )
    work = 4 * held * quarter * width
    keep, send = call(
        hidden_body,
        (jax.ShapeDtypeStruct(gate.shape, F32), jax.ShapeDtypeStruct(gate.shape, BF16)),
        [SCALAR, WHOLE, FAR, FAR],
        [pltpu.VMEM((CORES, width, quarter), BF16), pltpu.SemaphoreType.DMA((CORES,))],
        flops=work,
        moved=4 * quarter * width,
    )(core, arrived.reshape(CORES, experts, CAP, half), *far(w_down[0], down_other))
    away = lax.ppermute(send, "tensor", CHIP_SWAP)
    mask, w_both = call(
        functools.partial(prepare_body, experts=experts),
        (
            jax.ShapeDtypeStruct((2 * tokens, CORES * slots), BF16),
            jax.ShapeDtypeStruct((CORES, quarter, width), BF16),
        ),
        [WHOLE, ANY, FAR, FAR],
        [pltpu.SemaphoreType.DMA((CORES,))],
        flops=2 * tokens * slots * experts,
        moved=4 * quarter * width,
    )(ids, keep, *far(w_up[0], up_other))
    slot_grad = call(
        slot_grad_body,
        jax.ShapeDtypeStruct((CORES, experts // 2, 2, CAP, half), BF16),
        [SCALAR] + [WHOLE] * 4 + [ANY],
        flops=work,
        moved=4 * quarter * width,
    )(core, keep, away, gate, w_both, mask)
    back = exchange(slot_grad)
    moe_grad = call(
        combine_body,
        jax.ShapeDtypeStruct((tokens, quarter), BF16),
        [WHOLE] * 2,
        flops=4 * slots * tokens * quarter,
        moved=2 * slots * quarter,
    )(mask, back.reshape(CORES * slots, half))
    return (moe_grad, shared_grad)


def solution(mesh):
    placed = (
        P(("dp", "expert"), "tensor"),
        P(("dp", "expert"), None),
        P(("dp", "expert"), None),
        P("dp", "expert", None, None),
        P("expert", "tensor", None),
        P("expert", None, "tensor"),
        P(("dp", "expert"), None),
        P("tensor", None),
        P(None, "tensor"),
    )
    return jax.shard_map(
        on_device,
        mesh=mesh,
        in_specs=placed,
        out_specs=(P(("dp", "expert"), "tensor"), P(("dp", "expert"), "tensor")),
        check_vma=False,
    )
```
